128 devices in a mesh: gx: 8 (over z, core), gy: 16 (over x, y).
Axes of the slice: x: 4, y: 4, z: 4, core: 2. Of those that a mesh axis runs over, the one named last changes fastest.
Arguments:
- forward_fields: bfloat16 [2, 3, 3, 8, 768, 6144], P(None, None, None, None, 'gx', 'gy'), may hold values from -6 to 6
- adjoint_fields: bfloat16 [2, 3, 3, 8, 768, 6144], P(None, None, None, None, 'gx', 'gy'), may hold values from -6 to 6
- wave_weights: float32 [2, 3], replicated, may hold values from -4 to 4
- density: float32 [8, 512, 4096], P(None, 'gx', 'gy'), may hold values from 0 to 1
- row_edges: int32 [9], replicated, may hold values from 0 to 512, as said below
- column_edges: int32 [17], replicated, may hold values from 0 to 4096, as said below
Outputs:
- design_gradient: float32 [8, 512, 4096], P(None, 'gx', 'gy')
The draws below stay inside these ranges and needn't reach their ends.
Inputs may be any that keep to these rules, and one draw needn't show every extreme that they name: row_edges rises from 0 to 512; entry i lies within 16 of i * 64, so every group spans 32 to 96 cells along x, and some group spans exactly 96. column_edges rises from 0 to 4096; entry j lies within 64 of j * 256, so every group spans 128 to 384 cells along y, and some group spans exactly 384.
All inputs are finite; a program needn't handle non-finite values.
Results may differ from the reference program's by a relative error of at most 0.0003.
Values sent between devices are 32-bit elements; how exact they have to be, the bound alone decides.
No kernel may reach another device: no remote copies, remote signals or barrier semaphores. Data moves between devices by JAX's collectives and lax.ppermute only.
A program may use at most 192 MiB of HBM per device.

```python
import jax
import jax.numpy as jnp
from jax import lax

TX = 64
TY = 256
Z = 8
WAVES = 3
COMPS = 3
RADIUS = 10
CX = 96
CY = 384
NX = 512
NY = 4096
XC = 768
YC = 6144
N_GX = 8
N_GY = 16


def group_edges(key, number, tile_cells):
    shift_key, pick_key = jax.random.split(key)
    quarter = tile_cells // 4
    shifts = jax.random.randint(shift_key, (number + 1,), -quarter, quarter + 1)
    chosen = jax.random.randint(pick_key, (), 1, number - 1)
    positions = jnp.arange(number + 1)
    shifts = jnp.where(positions == chosen, -quarter, shifts)
    shifts = jnp.where(positions == chosen + 1, quarter, shifts)
    shifts = jnp.where((positions == 0) | (positions == number), 0, shifts)
    return (positions * tile_cells + shifts).astype(jnp.int32)


def draw_row_edges(key, part):
    key = jax.random.fold_in(key, 11)
    return group_edges(key, N_GX, TX)


def draw_column_edges(key, part):
    key = jax.random.fold_in(key, 12)
    return group_edges(key, N_GY, TY)


def steps_of(key, shape, cuts, least, top_value):
    factor_of, own = 1.0, jax.random.fold_in(key, 6)
    for axis_at, blocks in cuts:
        steps = jnp.exp(jax.random.uniform(jax.random.fold_in(own, axis_at), (blocks,), jnp.float32, least / len(cuts), top_value / len(cuts)))
        factor_of = factor_of * jnp.repeat(steps, shape[axis_at] // blocks).reshape([-1 if axis == axis_at else 1 for axis in range(len(shape))])
    return factor_of


def noise(stream_key, shape, deviation, reach, pieces=(), kind=jnp.bfloat16):
    values = jax.random.normal(stream_key, shape, jnp.float32) * deviation
    if len(pieces) > 0:
        values = steps_of(stream_key, shape, pieces, -0.22, 0.18) * values
    return jnp.clip(values, min=-reach, max=reach).astype(kind)


def setup_inputs(seed: int = 0) -> dict:
    seeds = jax.random.split(jax.random.key(seed), 7)
    forward_fields = noise(seeds[0], (2, WAVES, COMPS, Z, XC, YC), 1.0, 6.0, ((4, 8), (5, 16)))
    adjoint_fields = noise(seeds[1], (2, WAVES, COMPS, Z, XC, YC), 1.0, 6.0, ((4, 8), (5, 16)))
    wave_weights = noise(seeds[2], (2, WAVES), 1.0, 4.0, (), jnp.float32)
    density = jnp.clip(1.0 * jax.random.uniform(seeds[3], (Z, NX, NY), jnp.float32) ** steps_of(seeds[3], (Z, NX, NY), ((1, 8), (2, 16)), -0.2, 0.2), 0.0, 1.0)
    row_edges = draw_row_edges(jax.random.fold_in(seeds[6], 71), 0)
    column_edges = draw_column_edges(jax.random.fold_in(seeds[6], 71), 0)
    return {"forward_fields": forward_fields, "adjoint_fields": adjoint_fields, "wave_weights": wave_weights, "density": density, "row_edges": row_edges, "column_edges": column_edges}


BETA = 64.0
ETA = 0.5

def cone_table(radius):
    offsets = jnp.arange(-radius, radius + 1).astype(jnp.float32)
    distance = jnp.sqrt(offsets[:, None] * offsets[:, None] + offsets[None, :] * offsets[None, :])
    cone = jnp.maximum(1.0 - distance / radius, 0.0)
    return cone / jnp.sum(cone)

def cone_filter(field, kernel, radius):
    result = lax.conv_general_dilated(field[:, None], kernel[None, None], (1, 1), [(radius, radius), (radius, radius)], precision=lax.Precision.HIGHEST)
    return result[:, 0]

def slope_of(filtered):
    denominator = jnp.tanh(BETA * ETA) + jnp.tanh(BETA * (1.0 - ETA))
    inner = jnp.tanh(BETA * (filtered - ETA))
    return BETA * (1.0 - inner * inner) / denominator

def correlate(forward, adjoint, wave_weights):
    fwd_real = forward[0].astype(jnp.float32)
    fwd_imag = forward[1].astype(jnp.float32)
    adj_real = adjoint[0].astype(jnp.float32)
    adj_imag = adjoint[1].astype(jnp.float32)
    real_part = lax.optimization_barrier(jnp.sum(fwd_real * adj_real - fwd_imag * adj_imag, axis=1))
    imag_part = lax.optimization_barrier(jnp.sum(fwd_real * adj_imag + fwd_imag * adj_real, axis=1))
    broadcast_shape = (wave_weights.shape[1],) + (1,) * (real_part.ndim - 1)
    weighted = wave_weights[0].reshape(broadcast_shape) * real_part - wave_weights[1].reshape(broadcast_shape) * imag_part
    return lax.optimization_barrier(jnp.sum(weighted, axis=0))

def source_index(edges, number, capacity, total):
    cells = jnp.arange(total).astype(jnp.int32)
    owner = lax.optimization_barrier(jnp.sum((edges[1:number][None, :] <= cells[:, None]).astype(jnp.int32), axis=1))
    return owner * capacity + cells - edges[owner]

def reference(forward_fields, adjoint_fields, wave_weights, density, row_edges, column_edges):

    def group_row(index):
        forward = lax.dynamic_slice_in_dim(forward_fields, index * CX, CX, 4)
        adjoint = lax.dynamic_slice_in_dim(adjoint_fields, index * CX, CX, 4)
        return correlate(forward, adjoint, wave_weights)
    rows_all = lax.map(group_row, jnp.arange(N_GX).astype(jnp.int32))
    buffers = jnp.moveaxis(rows_all, 0, 1).reshape(Z, N_GX * CX, N_GY * CY)
    gradient = jnp.take(buffers, source_index(row_edges, N_GX, CX, NX), axis=1)
    gradient = jnp.take(gradient, source_index(column_edges, N_GY, CY, NY), axis=2)
    kernel = cone_table(RADIUS)
    filtered = cone_filter(density, kernel, RADIUS)
    return cone_filter(slope_of(filtered) * gradient, kernel, RADIUS)
```

```python
import jax
import jax.numpy as jnp
import ml_dtypes
import numpy as np
from jax import lax
from jax.experimental import pallas as pl
from jax.experimental.pallas import tpu as pltpu
from jax.sharding import PartitionSpec as P

RADIUS = 10
SETTINGS = 10
REACH = RADIUS - 1
TAPS = 2 * REACH + 1
BETA = 64.0
ETA = 0.5
LANES = 128
LAYERS = 8
LAGS = (TAPS + 1) // 2
ROWS, COLS = 64, 256
GROUP_ROWS, GROUP_COLS = 96, 384
ROW_SLACK, COL_SLACK = 16, 64
FRAME_ROWS = GROUP_ROWS + 2 * ROW_SLACK
SIDE = ROW_SLACK + REACH
FIRST = ROW_SLACK - REACH
NEED = ROWS + 2 * REACH
HALO = 2 * REACH
NINES = LANES // REACH
GROUPED = (ROWS + 2 * HALO) // 4
SPAN = LANES - 2 * REACH
SLOPE_PAIRS = NEED // 2 + 1
DENSITY_PAIRS = (NEED + HALO) // 2 + 2
F32 = jnp.float32
BF16 = jnp.bfloat16


def cone_blocks():
    offsets = np.arange(-RADIUS, RADIUS + 1).astype(np.float64)
    cone = np.maximum(1.0 - np.sqrt(offsets[:, None] ** 2 + offsets[None, :] ** 2) / RADIUS, 0.0)
    cone = (cone / cone.sum())[1:-1, 1:-1]
    blocks = np.zeros((LAGS, 2, LANES, 2, LANES))
    lanes = np.arange(REACH, LANES - REACH)
    for lag in range(LAGS):
        for source in range(2):
            for target in range(2):
                a = 2 * lag + source - target
                if 0 <= a < TAPS:
                    for b in range(TAPS):
                        blocks[lag, source, lanes + b - REACH, target, lanes] = cone[a, b]
    blocks = blocks.reshape(LAGS * 2 * LANES, 2 * LANES)
    high = blocks.astype(ml_dtypes.bfloat16)
    low = (blocks - high.astype(np.float64)).astype(ml_dtypes.bfloat16)
    return high, low


def lane_of(rows):
    return lax.broadcasted_iota(jnp.int32, (rows, LANES), 1)


def turn(value, shift):
    return pltpu.roll(value, shift % LANES, 1)


def place():
    i, j = lax.axis_index("gx"), lax.axis_index("gy")
    return i, j, lax.rem(i, 2), lax.rem(j, 2)


def sides_of():
    i, j = lax.axis_index("gx"), lax.axis_index("gy")
    return i > 0, i < lax.axis_size("gx") - 1, j > 0, j < lax.axis_size("gy") - 1


def chosen(parity, first, second):
    return jnp.where(parity == 0, first, second)


def row_at(e):
    return slice(e * LAYERS, (e + 1) * LAYERS)


def pair_at(e):
    return row_at(e // 2), slice((e % 2) * LANES, (e % 2 + 1) * LANES)


def start_kernel(flat, weights, rows, cols, xe, xo, tiles, settings, w_smem, r_smem, c_smem, sems):
    i, j, pi, pj = place()
    copies = [
        pltpu.make_async_copy(flat.at[:, 0:LANES], tiles.at[0], sems.at[0]),
        pltpu.make_async_copy(flat.at[:, LANES:COLS], tiles.at[1], sems.at[1]),
        pltpu.make_async_copy(weights, w_smem, sems.at[2]),
        pltpu.make_async_copy(rows, r_smem, sems.at[3]),
        pltpu.make_async_copy(cols, c_smem, sems.at[4]),
    ]
    for copy in copies:
        copy.start()
    for copy in copies:
        copy.wait()
    settings[0] = (r_smem[i] - i * ROWS + ROW_SLACK).astype(F32)
    settings[1] = (c_smem[j] - j * COLS + COL_SLACK).astype(F32)
    settings[2] = (r_smem[i + 1] - r_smem[i]).astype(F32)
    settings[3] = (c_smem[j + 1] - c_smem[j]).astype(F32)
    for part in range(2):
        for w in range(3):
            settings[4 + 3 * part + w] = w_smem[part, w]
    for parity, out in ((0, xe), (1, xo)):
        start = jnp.where(pi == parity, ROWS - HALO, 0)
        for r in range(HALO):
            for k in range(2):
                out[k, row_at(r), :] = tiles[k, pl.ds(start + r, LAYERS, stride=ROWS), :]


def correlate_kernel(forward, adjoint, settings, frame, xe, xo, fields, sems):
    i, j, pi, pj = place()

    def copies(n):
        return [
            pltpu.make_async_copy(source.at[:, :, :, n], fields.at[k, :, :, :, n], sems.at[k, n])
            for k, source in enumerate((forward, adjoint))
        ]

    for n in range(LAYERS):
        for copy in copies(n):
            copy.start()
    frame[...] = jnp.zeros_like(frame)
    down, across, span_rows, span_cols = [settings[n].astype(jnp.int32) for n in range(4)]
    weights = [[settings[4 + 3 * part + w] for w in range(3)] for part in range(2)]
    lane = lane_of(16)
    row = lax.broadcasted_iota(jnp.int32, (16, LANES), 0)
    turned = lax.rem(across, LANES)

    @pl.loop(0, LAYERS)
    def _(n):
        for copy in copies(n):
            copy.wait()
        for r in range(GROUP_ROWS // 16):
            before = jnp.zeros((16, LANES), F32)
            for k in range(3):
                at = (n, slice(16 * r, 16 * r + 16), slice(LANES * k, LANES * (k + 1)))
                total = None
                for w in range(3):
                    real = imag = None
                    for c in range(3):
                        fr = fields[(0, 0, w, c) + at].astype(F32)
                        fi = fields[(0, 1, w, c) + at].astype(F32)
                        ar = fields[(1, 0, w, c) + at].astype(F32)
                        ai = fields[(1, 1, w, c) + at].astype(F32)
                        re = fr * ar - fi * ai
                        im = fr * ai + fi * ar
                        real = re if real is None else real + re
                        imag = im if imag is None else imag + im
                    term = weights[0][w] * real - weights[1][w] * imag
                    total = term if total is None else total + term
                inside = (row < span_rows - 16 * r) & (lane < span_cols - LANES * k)
                total = pltpu.roll(jnp.where(inside, total, 0.0), turned, 1)
                value = jnp.where(lane >= across, total, before)
                before = total
                frame[k, pl.ds((16 * r + down) * LAYERS + n, 16, stride=LAYERS), :] = value

    for parity, out in ((0, xe), (1, xo)):
        start = pl.multiple_of(jnp.where(pi == parity, ROWS + FIRST, 0) * LAYERS, 8)
        out[...] = frame[:, pl.ds(start, SIDE * LAYERS), :]


def density_row(tiles, xe, xo, e, k):
    i, j, pi, pj = place()
    has_up, has_down, has_left, has_right = sides_of()
    if e >= ROWS + 2 * HALO:
        return jnp.zeros((LAYERS, LANES), F32)
    if HALO <= e < HALO + ROWS:
        return tiles[k, pl.ds(e - HALO, LAYERS, stride=ROWS), :]
    at = (k, row_at(e % (HALO + ROWS)))
    if e < HALO:
        return jnp.where(has_up, chosen(pi, xo[at], xe[at]), 0.0)
    return jnp.where(has_down, chosen(pi, xe[at], xo[at]), 0.0)


def density_columns_kernel(tiles, xe, xo, ye, yo):
    i, j, pi, pj = place()
    lane = lane_of(LAYERS)
    for r in range(GROUPED):
        left = right = None
        for g in range(4):
            a = turn(density_row(tiles, xe, xo, g * GROUPED + r, 0), 32 * g)
            b = turn(density_row(tiles, xe, xo, g * GROUPED + r, 1), 32 * g + 32)
            left = a if g == 0 else jnp.where(lane >= 32 * g, a, left)
            right = b if g == 0 else jnp.where(lane >= 32 * g, b, right)
        ye[row_at(r), :] = chosen(pj, right, left)
        yo[row_at(r), :] = chosen(pj, left, right)


def split_copies(windows, copies, pairs):
    for shift in range(2):
        for g in range((pairs - shift) // 2):
            value = windows[(2 * g + shift) * LAYERS : (2 * g + shift + 2) * LAYERS, :]
            high = value.astype(BF16)
            low = (value - high.astype(F32)).astype(BF16)
            copies[shift, 0, 16 * g : 16 * g + 16, :] = high
            copies[shift, 1, 16 * g : 16 * g + 16, :] = low


def banded(windows, copies, pairs, high_ref, low_ref, rows):
    split_copies(windows, copies, pairs)

    def part(kind):
        return jnp.concatenate(
            [copies[lag % 2, kind, 16 * (lag // 2) : 16 * (lag // 2) + rows, :] for lag in range(LAGS)], axis=1
        )

    high = part(0)
    out = jnp.dot(part(1), high_ref[...], preferred_element_type=F32)
    out += jnp.dot(high, low_ref[...], preferred_element_type=F32)
    return out + jnp.dot(high, high_ref[...], preferred_element_type=F32)


def slope_of(filtered):
    e = jnp.exp(-2.0 * BETA * jnp.abs(filtered - ETA))
    scale = 4.0 * BETA / (np.tanh(BETA * ETA) + np.tanh(BETA * (1.0 - ETA)))
    return np.float32(scale) * e / ((1.0 + e) * (1.0 + e))


def slope_middle_kernel(tiles, xe, xo, high_ref, low_ref, slope, windows, copies):
    lane = lane_of(LAYERS)
    for e in range(2 * DENSITY_PAIRS):
        t0, t1 = [density_row(tiles, xe, xo, e, k) for k in range(2)]
        windows[pair_at(e)] = jnp.where(lane < 64, turn(t0, 64), turn(t1, 64))
    slope[...] = slope_of(banded(windows, copies, DENSITY_PAIRS, high_ref, low_ref, SLOPE_PAIRS * LAYERS))


def slope_sides_kernel(tiles, xe, xo, ye, yo, high_ref, low_ref, left_slope, right_slope, windows, copies):
    i, j, pi, pj = place()
    has_up, has_down, has_left, has_right = sides_of()
    lane = lane_of(LAYERS)
    for e in range(2 * DENSITY_PAIRS):
        g, r = divmod(min(e, 4 * GROUPED - 1), GROUPED)
        at = row_at(r)
        left = turn(jnp.where(has_left, chosen(pj, yo[at, :], ye[at, :]), 0.0), 28 - 14 - 32 * g)
        right = turn(jnp.where(has_right, chosen(pj, ye[at, :], yo[at, :]), 0.0), 82 - 32 * g)
        t0, t1 = [turn(density_row(tiles, xe, xo, e, k), 46 - 92 * k) for k in range(2)]
        windows[(0,) + pair_at(e)] = jnp.where(lane >= 46, t0, jnp.where(lane >= 28, left, 0.0))
        windows[(1,) + pair_at(e)] = jnp.where(lane < 82, t1, jnp.where(lane < 100, right, 0.0))
    for n, out in enumerate((left_slope, right_slope)):
        value = banded(windows.at[n], copies.at[n], DENSITY_PAIRS, high_ref, low_ref, SLOPE_PAIRS * LAYERS)
        out[...] = slope_of(value)


def side_rows(count):
    return -(-count // 2), -(-count // NINES)


def add_rows(frame, xe, xo, tiles):
    i, j, pi, pj = place()
    has_up, has_down, has_left, has_right = sides_of()
    size = SIDE * LAYERS
    for k in tiles:
        frame[k, FIRST * LAYERS : FIRST * LAYERS + size, :] += jnp.where(has_up, chosen(pi, xo[k], xe[k]), 0.0)
        frame[k, ROWS * LAYERS : ROWS * LAYERS + size, :] += jnp.where(has_down, chosen(pi, xe[k], xo[k]), 0.0)


def columns_kernel(own, xe, xo, ye, yo, frame):
    i, j, pi, pj = place()
    for k in (0, 2):
        frame[k] = own[k, 0 : GROUP_ROWS * LAYERS, :]
    add_rows(frame, xe, xo, (0, 2))
    half, nine = side_rows(NEED)
    upper, lower = lane_of(half * LAYERS), lane_of(nine * LAYERS)
    for parity, out in ((0, ye), (1, yo)):
        right = pj == parity
        tile = jnp.where(right, 2, 0)
        first = frame[tile, FIRST * LAYERS : (FIRST + half) * LAYERS, :]
        second = frame[tile, (FIRST + half) * LAYERS : (FIRST + 2 * half) * LAYERS, :]
        swing = jnp.where(right, 0, 64)
        out[0 : half * LAYERS, :] = jnp.where(upper >= 64, pltpu.roll(first, swing, 1), pltpu.roll(second, 64 - swing, 1))
        packed = jnp.zeros((nine * LAYERS, LANES), F32)
        base = jnp.where(right, LANES - 55, 64)
        for g in range(NINES):
            value = frame[tile, (FIRST + nine * g) * LAYERS : (FIRST + nine * (g + 1)) * LAYERS, :]
            value = pltpu.roll(value, lax.rem(base + REACH * g, LANES), 1)
            packed = jnp.where((lower >= REACH * g) & (lower < REACH * g + REACH), value, packed)
        out[half * LAYERS : (half + nine) * LAYERS, :] = packed


def side_unpack(frame, packed, tile, valid):
    half, nine = side_rows(NEED)
    from_left = tile == 0
    lane = lane_of(half * LAYERS)
    keep = ((lane >= 64) if from_left else (lane < 64)) & valid
    value = packed(0, half * LAYERS)
    for h in range(2):
        at = pl.ds((FIRST + h * half) * LAYERS, half * LAYERS)
        shown = turn(value, 64) if (h == 0) != from_left else value
        frame[tile, at, :] += jnp.where(keep, shown, 0.0)
    lane = lane_of(nine * LAYERS)
    value = packed(half * LAYERS, nine * LAYERS)
    start = 55 if from_left else 64
    keep = (lane >= start) & (lane < start + REACH) & valid
    for g in range(NINES):
        at = pl.ds((FIRST + nine * g) * LAYERS, nine * LAYERS)
        frame[tile, at, :] += jnp.where(keep, turn(value, start - REACH * g), 0.0)


def gradient_middle_kernel(own, xe, xo, left_slope, slope, right_slope, high_ref, low_ref, out, frame, windows, copies):
    lane = lane_of(LAYERS)
    frame[1] = own[1, 0 : GROUP_ROWS * LAYERS, :]
    add_rows(frame, xe, xo, (1,))
    for e in range(2 * SLOPE_PAIRS):
        at = pair_at(e)
        factor = jnp.where(lane < REACH, turn(left_slope[at], -SPAN), slope[at])
        factor = jnp.where(lane < LANES - REACH, factor, turn(right_slope[at], SPAN))
        windows[at] = frame[1, row_at(FIRST + e), :] * factor
    out[...] = banded(windows, copies, SLOPE_PAIRS, high_ref, low_ref, ROWS // 2 * LAYERS)


def gradient_sides_kernel(
    own, xe, xo, ye, yo, left_slope, slope, right_slope, middle, high_ref, low_ref, out, frame, windows, copies, result
):
    i, j, pi, pj = place()
    has_up, has_down, has_left, has_right = sides_of()
    frame[...] = own[:, 0 : GROUP_ROWS * LAYERS, :]
    add_rows(frame, xe, xo, range(3))

    def pick(first, second):
        return lambda at, count: chosen(pj, first[at : at + count, :], second[at : at + count, :])

    side_unpack(frame, pick(yo, ye), 0, has_left)
    side_unpack(frame, pick(ye, yo), 2, has_right)
    lane = lane_of(LAYERS)
    for e in range(2 * SLOPE_PAIRS):
        at = pair_at(e)
        t0, t1, t2 = [frame[k, row_at(FIRST + e), :] for k in range(3)]
        factor = jnp.where(lane < LANES - REACH, left_slope[at], turn(slope[at], SPAN))
        windows[(0,) + at] = jnp.where(lane < 110, turn(t0, -18), turn(t1, -18)) * factor
        factor = jnp.where(lane < REACH, turn(slope[at], -SPAN), right_slope[at])
        windows[(1,) + at] = jnp.where(lane < 18, turn(t1, 18), turn(t2, 18)) * factor
    for n in range(2):
        result[n] = banded(windows.at[n], copies.at[n], SLOPE_PAIRS, high_ref, low_ref, ROWS // 2 * LAYERS)
    for e in range(ROWS):
        at = pair_at(e)
        mid = turn(middle[at], 64)
        frame[0, row_at(e), :] = jnp.where(lane < 73, turn(result[(0,) + at], -46), mid)
        frame[1, row_at(e), :] = jnp.where(lane < 55, mid, turn(result[(1,) + at], 46))
    for z in range(LAYERS):
        for k in range(2):
            out[z, :, LANES * k : LANES * (k + 1)] = frame[k, pl.ds(z, ROWS, stride=LAYERS), :]


def partner(index, count, parity):
    other = index ^ 1 if parity == 0 else ((index - 1) ^ 1) + 1
    return other if 0 <= other < count else None


def exchange(pair, axis):
    nx, ny = lax.axis_size("gx"), lax.axis_size("gy")
    arrived = []
    for parity, value in enumerate(pair):
        moves = []
        for i in range(nx):
            for j in range(ny):
                to = (partner(i, nx, parity), j) if axis == "gx" else (i, partner(j, ny, parity))
                if None in to:
                    to = (i, j ^ 1) if axis == "gx" else (i ^ 1, j)
                moves.append((i * ny + j, to[0] * ny + to[1]))
        arrived.append(lax.ppermute(value, ("gx", "gy"), moves))
    return arrived


ANY = pl.BlockSpec(memory_space=pl.ANY)
SMEM = pl.BlockSpec(memory_space=pltpu.SMEM)
VMEM = pl.BlockSpec(memory_space=pltpu.VMEM)


def shaped(*shape):
    return jax.ShapeDtypeStruct(shape, F32)


def call(kernel, name, ins, outs, scratch, mib, flops, moved):
    return pl.pallas_call(
        kernel,
        out_shape=outs,
        in_specs=ins,
        out_specs=jax.tree.map(lambda s: SMEM if s.shape == (SETTINGS,) else VMEM, outs),
        scratch_shapes=scratch,
        compiler_params=pltpu.CompilerParams(vmem_limit_bytes=mib << 20),
        cost_estimate=pl.CostEstimate(flops=int(flops), bytes_accessed=int(moved * (1 << 20)), transcendentals=0),
        name=name,
    )


def body(forward, adjoint, weights, density, row_edges, column_edges):
    high, low = (jnp.asarray(m) for m in cone_blocks())
    forward, adjoint, flat, weights, row_edges, column_edges = [
        pltpu.with_memory_space_constraint(x, pltpu.HBM)
        for x in (forward, adjoint, density.reshape(LAYERS * ROWS, COLS), weights, row_edges, column_edges)
    ]
    halo = shaped(2, HALO * LAYERS, LANES)
    tile = shaped(2, LAYERS * ROWS, LANES)
    whole_frame = shaped(3, FRAME_ROWS * LAYERS, LANES)
    fields = pltpu.VMEM((2, 2, 3, 3, LAYERS, GROUP_ROWS, GROUP_COLS), BF16)
    sems = pltpu.SemaphoreType.DMA((2, LAYERS))
    xe, xo, tiles, settings = call(
        start_kernel,
        "start",
        [ANY] * 4,
        [halo, halo, tile, shaped(SETTINGS)],
        [
            pltpu.SMEM((2, 3), F32),
            pltpu.SMEM(row_edges.shape, jnp.int32),
            pltpu.SMEM(column_edges.shape, jnp.int32),
            pltpu.SemaphoreType.DMA((5,)),
        ],
        2,
        0,
        1,
    )(flat, weights, row_edges, column_edges)
    halo_rows = exchange((xe, xo), "gx")

    side = shaped(3, SIDE * LAYERS, LANES)
    frame, *own_rows = call(
        correlate_kernel, "correlate", [ANY, ANY, SMEM], [whole_frame, side, side], [fields, sems], 28, 0, 24
    )(forward, adjoint, settings)
    own_rows = exchange(own_rows, "gx")

    column = shaped(GROUPED * LAYERS, LANES)
    halo_columns = call(density_columns_kernel, "density_columns", [VMEM] * 3, [column, column], [], 2, 0, 30)(
        tiles, *halo_rows
    )
    halo_columns = exchange(halo_columns, "gy")

    def work(pairs, windows):
        lead = () if windows == 1 else (windows,)
        return [
            pltpu.VMEM(lead + (pairs * LAYERS, 2 * LANES), F32),
            pltpu.VMEM(lead + (2, 2, pairs * LAYERS, 2 * LANES), BF16),
        ]

    slope = shaped(SLOPE_PAIRS * LAYERS, 2 * LANES)
    middle_slope = call(
        slope_middle_kernel, "slope_middle", [VMEM] * 5, slope, work(DENSITY_PAIRS, 1), 8, 1.3e9, 30
    )(tiles, *halo_rows, high, low)
    left_slope, right_slope = call(
        slope_sides_kernel, "slope_sides", [VMEM] * 7, [slope, slope], work(DENSITY_PAIRS, 2), 8, 2.6e9, 4
    )(tiles, *halo_rows, *halo_columns, high, low)

    own_frame = pltpu.VMEM((3, GROUP_ROWS * LAYERS, LANES), F32)
    packed = shaped(sum(side_rows(NEED)) * LAYERS, LANES)
    own_columns = call(columns_kernel, "columns", [VMEM] * 3, [packed, packed], [own_frame], 4, 0, 4)(frame, *own_rows)
    own_columns = exchange(own_columns, "gy")

    middle = call(
        gradient_middle_kernel,
        "gradient_middle",
        [VMEM] * 8,
        shaped(ROWS // 2 * LAYERS, 2 * LANES),
        [own_frame] + work(SLOPE_PAIRS, 1),
        8,
        1e9,
        4,
    )(frame, *own_rows, left_slope, middle_slope, right_slope, high, low)
    return call(
        gradient_sides_kernel,
        "gradient_sides",
        [VMEM] * 11,
        shaped(*density.shape),
        [own_frame] + work(SLOPE_PAIRS, 2) + [pltpu.VMEM((2, ROWS // 2 * LAYERS, 2 * LANES), F32)],
        12,
        2e9,
        4,
    )(frame, *own_rows, *own_columns, left_slope, middle_slope, right_slope, middle, high, low)


def solution(mesh):
    placed = (
        P(None, None, None, None, "gx", "gy"),
        P(None, None, None, None, "gx", "gy"),
        P(),
        P(None, "gx", "gy"),
        P(),
        P(),
    )
    return jax.shard_map(body, mesh=mesh, in_specs=placed, out_specs=P(None, "gx", "gy"), check_vma=False)
```

```python
import jax
import jax.numpy as jnp
import ml_dtypes
import numpy as np
from jax import lax
from jax.experimental import pallas as pl
from jax.experimental.pallas import tpu as pltpu
from jax.sharding import PartitionSpec as P

RADIUS = 10
REACH = RADIUS - 1
TAPS = 2 * REACH + 1
BETA = 64.0
ETA = 0.5
LANES = 128
LAYERS = 8
QUAD = 4
PIECE = 64
SPAN = PIECE - 2 * REACH
LAGS = 6
ROWS, COLS = 64, 256
GROUP_ROWS, GROUP_COLS = 96, 384
ROW_SLACK, COL_SLACK = 16, 64
FRAME_ROWS = GROUP_ROWS + 2 * ROW_SLACK
SIDE = ROW_SLACK + REACH
FIRST = ROW_SLACK - REACH
NEED = ROWS + 2 * REACH
HALO = 2 * REACH
GROUPS = LANES // HALO
GROUPED = -(-(ROWS + 2 * HALO) // GROUPS)
INNER = (SIDE + FIRST, ROWS)
HALF = (INNER[1] - INNER[0]) // 2
WINDOWS = 6
STARTS = [SPAN * w - HALO for w in range(WINDOWS)]
MIDDLE_SLOPES = (1, 2, 3, 4)
MIDDLE = (2, 3)
SLOPE_ROWS = 176
DENSITY_QUADS = SLOPE_ROWS // LAYERS + LAGS - 1
GRADIENT_ROWS = ROWS // QUAD * LAYERS
GRADIENT_QUADS = ROWS // QUAD + LAGS - 1
CHUNK = GROUP_ROWS // 2
F32 = jnp.float32
BF16 = jnp.bfloat16


def cone_blocks():
    offsets = np.arange(-RADIUS, RADIUS + 1).astype(np.float64)
    cone = np.maximum(1.0 - np.sqrt(offsets[:, None] ** 2 + offsets[None, :] ** 2) / RADIUS, 0.0)
    cone = (cone / cone.sum())[1:-1, 1:-1]
    blocks = np.zeros((LAGS, QUAD, PIECE, QUAD, PIECE))
    lanes = np.arange(2 * REACH, PIECE)
    for lag in range(LAGS):
        for source in range(QUAD):
            for target in range(QUAD):
                a = QUAD * lag + source - target
                if 0 <= a < TAPS:
                    for b in range(TAPS):
                        blocks[lag, source, lanes + b - 2 * REACH, target, lanes] = cone[a, b]
    blocks = blocks.reshape(LAGS * QUAD * PIECE, QUAD * PIECE)
    high = blocks.astype(ml_dtypes.bfloat16)
    low = (blocks - high.astype(np.float64)).astype(ml_dtypes.bfloat16)
    return high, low


def lane_of(rows):
    return lax.broadcasted_iota(jnp.int32, (rows, LANES), 1)


def turn(value, shift):
    return pltpu.roll(value, shift % LANES, 1)


def place():
    i, j = lax.axis_index("gx"), lax.axis_index("gy")
    return i, j, lax.rem(i, 2), lax.rem(j, 2)


def sides_of():
    i, j = lax.axis_index("gx"), lax.axis_index("gy")
    return i > 0, i < lax.axis_size("gx") - 1, j > 0, j < lax.axis_size("gy") - 1


def chosen(parity, first, second):
    return jnp.where(parity == 0, first, second)


def row_at(e):
    return slice(e * LAYERS, (e + 1) * LAYERS)


def half_at(e):
    return row_at(e // QUAD), slice((e % QUAD) * PIECE, (e % QUAD) * PIECE + LANES)


def piece_of(tiles, start):
    k, first = divmod(start, LANES)
    value = tiles[k]
    if first > LANES - PIECE:
        value = jnp.where(lane_of(LAYERS) >= first, value, tiles[k + 1])
    return turn(value, -first), turn(value, PIECE - first)


def correlate_kernel(forward, adjoint, weights, rows, cols, frame, xe, xo, fields, w_smem, r_smem, c_smem, sems, small):
    i, j, pi, pj = place()
    scalars = [
        pltpu.make_async_copy(source, target, small.at[n])
        for n, (source, target) in enumerate(((weights, w_smem), (rows, r_smem), (cols, c_smem)))
    ]

    def copies(n):
        at = pl.ds(pl.multiple_of(lax.rem(n, 2) * CHUNK, CHUNK), CHUNK)
        return [
            pltpu.make_async_copy(source.at[:, :, :, lax.div(n, 2), at], fields.at[k, :, :, :, n], sems.at[k, n])
            for k, source in enumerate((forward, adjoint))
        ]

    for copy in scalars:
        copy.start()
    for n in range(2 * LAYERS):
        for copy in copies(jnp.int32(n)):
            copy.start()
    frame[...] = jnp.zeros_like(frame)
    for copy in scalars:
        copy.wait()
    down = r_smem[i] - i * ROWS + ROW_SLACK
    across = c_smem[j] - j * COLS + COL_SLACK
    span_rows = r_smem[i + 1] - r_smem[i]
    span_cols = c_smem[j + 1] - c_smem[j]
    lane = lane_of(16)
    row = lax.broadcasted_iota(jnp.int32, (16, LANES), 0)
    turned = lax.rem(across, LANES)

    @pl.loop(0, 2 * LAYERS)
    def _(n):
        for copy in copies(n):
            copy.wait()
        z, top = lax.div(n, 2), lax.rem(n, 2) * CHUNK
        for r in range(0, CHUNK, 16):
            before = jnp.zeros((16, LANES), F32)
            for k in range(3):
                at = (n, slice(r, r + 16), slice(LANES * k, LANES * (k + 1)))
                total = None
                for w in range(3):
                    real = imag = None
                    for c in range(3):
                        fr = fields[(0, 0, w, c) + at].astype(F32)
                        fi = fields[(0, 1, w, c) + at].astype(F32)
                        ar = fields[(1, 0, w, c) + at].astype(F32)
                        ai = fields[(1, 1, w, c) + at].astype(F32)
                        re = fr * ar - fi * ai
                        im = fr * ai + fi * ar
                        real = re if real is None else real + re
                        imag = im if imag is None else imag + im
                    term = w_smem[0, w] * real - w_smem[1, w] * imag
                    total = term if total is None else total + term
                inside = (row < span_rows - top - r) & (lane < span_cols - LANES * k)
                total = pltpu.roll(jnp.where(inside, total, 0.0), turned, 1)
                value = jnp.where(lane >= across, total, before)
                before = total
                frame[k, pl.ds((top + r + down) * LAYERS + z, 16, stride=LAYERS), :] = value

    for parity, out in ((0, xe), (1, xo)):
        start = pl.multiple_of(jnp.where(pi == parity, ROWS + FIRST, 0) * LAYERS, 8)
        out[...] = frame[:, pl.ds(start, SIDE * LAYERS), :]


def density_rows_kernel(flat, xe, xo, tiles, sems):
    i, j, pi, pj = place()
    copies = [pltpu.make_async_copy(flat.at[:, LANES * k : LANES * (k + 1)], tiles.at[k], sems.at[k]) for k in range(2)]
    for copy in copies:
        copy.start()
    for copy in copies:
        copy.wait()
    for parity, out in ((0, xe), (1, xo)):
        start = jnp.where(pi == parity, ROWS - HALO, 0)
        for r in range(HALO):
            for k in range(2):
                out[k, row_at(r), :] = tiles[k, pl.ds(start + r, LAYERS, stride=ROWS), :]


def density_row(tiles, xe, xo, e, k):
    i, j, pi, pj = place()
    has_up, has_down, has_left, has_right = sides_of()
    if e >= ROWS + 2 * HALO:
        return jnp.zeros((LAYERS, LANES), F32)
    if HALO <= e < HALO + ROWS:
        return tiles[k, pl.ds(e - HALO, LAYERS, stride=ROWS), :]
    at = (k, row_at(e % (HALO + ROWS)))
    if e < HALO:
        return jnp.where(has_up, chosen(pi, xo[at], xe[at]), 0.0)
    return jnp.where(has_down, chosen(pi, xe[at], xo[at]), 0.0)


def side_pack(frame, out, first_row, right, blocks, nines, count):
    tile = jnp.where(right, 2, 0)
    size = blocks[0][1] * LAYERS
    upper = lane_of(size)
    first, second = [frame[tile, at * LAYERS : at * LAYERS + size, :] for at, _ in blocks]
    swing = jnp.where(right, 0, 64)
    out[first_row : first_row + size, :] = jnp.where(
        upper >= 64, pltpu.roll(first, swing, 1), pltpu.roll(second, 64 - swing, 1)
    )
    lower = lane_of(count * LAYERS)
    packed = None
    base = jnp.where(right, LANES - 55, 64)
    for g, (at, _) in enumerate(nines):
        value = frame[tile, at * LAYERS : (at + count) * LAYERS, :]
        value = pltpu.roll(value, lax.rem(base + REACH * g, LANES), 1)
        packed = value if g == 0 else jnp.where(lower >= REACH * g, value, packed)
    out[first_row + size : first_row + size + count * LAYERS, :] = packed


def side_unpack(frame, packed, first_row, tile, valid, blocks, nines, count):
    from_left = tile == 0
    size = blocks[0][1] * LAYERS
    lane = lane_of(size)
    keep = ((lane >= 64) if from_left else (lane < 64)) & valid
    value = packed(first_row, size)
    for h, (at, _) in enumerate(blocks):
        shown = turn(value, 64) if (h == 0) != from_left else value
        frame[tile, at * LAYERS : at * LAYERS + size, :] += jnp.where(keep, shown, 0.0)
    value = packed(first_row + size, count * LAYERS)
    start = 55 if from_left else 64
    lane = lane_of(count * LAYERS)
    keep = (lane >= start) & (lane < start + REACH) & valid
    for g, (at, rows) in enumerate(nines):
        shown = jnp.where(keep, turn(value, start - REACH * g), 0.0)
        frame[tile, at * LAYERS : (at + rows) * LAYERS, :] += shown[0 : rows * LAYERS, :]


def split_rows(first, end, count):
    return [(at, min(count, end - at)) for at in range(first, end, count)]


INNER_SIDE = (((INNER[0], HALF), (INNER[0] + HALF, HALF)), split_rows(*INNER, 3), 3)
OUTER_SIDE = (((FIRST, SIDE), (ROWS, SIDE)), split_rows(FIRST, FIRST + SIDE, 4) + split_rows(ROWS, ROWS + SIDE, 4), 4)
DENSITY_PART = GROUPED * LAYERS


def side_size(side):
    return (side[0][0][1] + side[2]) * LAYERS


def first_columns_kernel(tiles, xe, xo, own, ye, yo):
    i, j, pi, pj = place()
    lane = lane_of(LAYERS)
    for r in range(GROUPED):
        left = right = None
        for g in range(GROUPS):
            a = turn(density_row(tiles, xe, xo, g * GROUPED + r, 0), HALO * g)
            b = turn(density_row(tiles, xe, xo, g * GROUPED + r, 1), HALO * g + HALO)
            left = a if g == 0 else jnp.where(lane >= HALO * g, a, left)
            right = b if g == 0 else jnp.where(lane >= HALO * g, b, right)
        ye[row_at(r), :] = chosen(pj, right, left)
        yo[row_at(r), :] = chosen(pj, left, right)
    for parity, out in ((0, ye), (1, yo)):
        side_pack(own, out, DENSITY_PART, pj == parity, *INNER_SIDE)


def banded(windows, copies, count, rows, high_ref, low_ref):
    size = rows + LAYERS * (LAGS - 2)
    for w in range(count):
        for shift in range(2):
            for r in range(0, size, 16):
                value = windows[w, r + shift * LAYERS : r + shift * LAYERS + 16, :]
                high = value.astype(BF16)
                copies[w, shift, 0, r : r + 16, :] = high
                copies[w, shift, 1, r : r + 16, :] = (value - high.astype(F32)).astype(BF16)

    def part(kind):
        return jnp.concatenate(
            [
                jnp.concatenate(
                    [copies[w, lag % 2, kind, 16 * (lag // 2) : 16 * (lag // 2) + rows, :] for lag in range(LAGS)],
                    axis=1,
                )
                for w in range(count)
            ],
            axis=0,
        )

    high = part(0)
    out = jnp.dot(part(1), high_ref[...], preferred_element_type=F32)
    out += jnp.dot(high, low_ref[...], preferred_element_type=F32)
    return out + jnp.dot(high, high_ref[...], preferred_element_type=F32)


def slope_of(filtered):
    e = jnp.exp(-2.0 * BETA * jnp.abs(filtered - ETA))
    scale = 4.0 * BETA / (np.tanh(BETA * ETA) + np.tanh(BETA * (1.0 - ETA)))
    return np.float32(scale) * e / ((1.0 + e) * (1.0 + e))


def store_slope(value, out, count):
    for w in range(count):
        out[w] = slope_of(value[w * SLOPE_ROWS : (w + 1) * SLOPE_ROWS, :])


def slope_middle_kernel(tiles, xe, xo, high_ref, low_ref, slope, windows, copies):
    lower = lane_of(LAYERS) < PIECE
    for e in range(0, QUAD * DENSITY_QUADS, 2):
        even, odd = [[density_row(tiles, xe, xo, e + h, k) for k in range(2)] for h in range(2)]
        for n, w in enumerate(MIDDLE_SLOPES):
            windows[(n,) + half_at(e)] = jnp.where(
                lower, piece_of(even, STARTS[w])[0], piece_of(odd, STARTS[w])[1]
            )
    count = len(MIDDLE_SLOPES)
    store_slope(banded(windows, copies, count, SLOPE_ROWS, high_ref, low_ref), slope, count)


def slope_sides_kernel(tiles, xe, xo, ye, yo, high_ref, low_ref, slope, windows, copies):
    i, j, pi, pj = place()
    has_up, has_down, has_left, has_right = sides_of()
    lane = lane_of(LAYERS)
    lower = lane < PIECE
    within = jnp.where(lower, lane, lane - PIECE)
    own_left, own_right = within >= HALO, within < COLS - STARTS[-1]
    edge = within < COLS - STARTS[-1] + HALO
    for e in range(0, QUAD * DENSITY_QUADS, 2):
        lefts, rights = [], []
        for h in range(2):
            g, r = divmod(min(e + h, GROUPS * GROUPED - 1), GROUPED)
            at = row_at(r)
            left = jnp.where(has_left, chosen(pj, yo[at, :], ye[at, :]), 0.0)
            right = jnp.where(has_right, chosen(pj, ye[at, :], yo[at, :]), 0.0)
            left = turn(left, PIECE * h - HALO * g)
            right = turn(right, PIECE * h + COLS - STARTS[-1] - HALO * g)
            t0, t1 = [density_row(tiles, xe, xo, e + h, k) for k in range(2)]
            lefts.append(jnp.where(own_left, turn(t0, PIECE * h - STARTS[0]), left))
            rights.append(
                jnp.where(own_right, turn(t1, PIECE * h + LANES - STARTS[-1]), jnp.where(edge, right, 0.0))
            )
        windows[(0,) + half_at(e)] = jnp.where(lower, *lefts)
        windows[(1,) + half_at(e)] = jnp.where(lower, *rights)
    store_slope(banded(windows, copies, 2, SLOPE_ROWS, high_ref, low_ref), slope, 2)


def add_rows(frame, xe, xo, tiles):
    i, j, pi, pj = place()
    has_up, has_down, has_left, has_right = sides_of()
    size = SIDE * LAYERS
    for k in tiles:
        frame[k, FIRST * LAYERS : FIRST * LAYERS + size, :] += jnp.where(has_up, chosen(pi, xo[k], xe[k]), 0.0)
        frame[k, ROWS * LAYERS : ROWS * LAYERS + size, :] += jnp.where(has_down, chosen(pi, xe[k], xo[k]), 0.0)


def columns_kernel(own, xe, xo, ye, yo, frame):
    i, j, pi, pj = place()
    for k in (0, 2):
        frame[k] = own[k, 0 : GROUP_ROWS * LAYERS, :]
    add_rows(frame, xe, xo, (0, 2))
    for parity, out in ((0, ye), (1, yo)):
        side_pack(frame, out, 0, pj == parity, *OUTER_SIDE)


def add_columns(frame, ye, yo, first_row, side):
    i, j, pi, pj = place()
    has_up, has_down, has_left, has_right = sides_of()

    def pick(first, second):
        return lambda at, count: chosen(pj, first[at : at + count, :], second[at : at + count, :])

    side_unpack(frame, pick(yo, ye), first_row, 0, has_left, *side)
    side_unpack(frame, pick(ye, yo), first_row, 2, has_right, *side)


def weigh(frame, windows, n, w, slope, before):
    lane = lane_of(LAYERS)
    lower = lane < PIECE
    own = jnp.where(lower, lane, lane - PIECE) >= 2 * REACH
    for e in range(0, QUAD * GRADIENT_QUADS, 2):
        at = half_at(e)
        even, odd = [[frame[k, row_at(FIRST + e + h), :] for k in range(3)] for h in range(2)]
        start = STARTS[w] - REACH + COL_SLACK
        factor = slope[at] if before is None else jnp.where(own, slope[at], turn(before[at], -SPAN))
        windows[(n,) + at] = jnp.where(lower, piece_of(even, start)[0], piece_of(odd, start)[1]) * factor


def gradient_middle_kernel(own, xe, xo, ye, yo, slope, high_ref, low_ref, out, frame, windows, copies):
    frame[...] = own[:, 0 : GROUP_ROWS * LAYERS, :]
    add_rows(frame, xe, xo, range(3))
    for n, w in enumerate(MIDDLE):
        weigh(frame, windows, n, w, slope.at[w - 1], slope.at[w - 2])
    out[...] = banded(windows, copies, len(MIDDLE), GRADIENT_ROWS, high_ref, low_ref)
    add_columns(frame, ye, yo, DENSITY_PART, INNER_SIDE)


def gradient_sides_kernel(given, ye, yo, slope, outer, middle, high_ref, low_ref, out, frame, windows, copies, result):
    frame[...] = given[...]
    add_columns(frame, ye, yo, 0, OUTER_SIDE)
    weigh(frame, windows, 0, 0, outer.at[0], None)
    weigh(frame, windows, 1, 1, slope.at[0], outer.at[0])
    weigh(frame, windows, 2, 4, slope.at[3], slope.at[2])
    weigh(frame, windows, 3, 5, outer.at[1], slope.at[3])
    result[...] = banded(windows, copies, 4, GRADIENT_ROWS, high_ref, low_ref)
    lane = lane_of(LAYERS)
    places = ((result, 0), (result, 1), (middle, 0), (middle, 1), (result, 2), (result, 3))
    for e in range(ROWS):
        rows, lanes = half_at(e - e % 2)
        pieces = []
        for w, (source, n) in enumerate(places):
            at = slice(rows.start + n * GRADIENT_ROWS, rows.stop + n * GRADIENT_ROWS)
            pieces.append(turn(source[at, lanes], STARTS[w] - 2 * REACH - PIECE * (e % 2)))
        for k in range(2):
            value = None
            for w, piece in enumerate(pieces):
                first = STARTS[w] - LANES * k
                if first < LANES and first + SPAN > 0:
                    value = piece if value is None else jnp.where(lane >= first, piece, value)
            frame[k, row_at(e), :] = value
    for z in range(LAYERS):
        for k in range(2):
            out[z, :, LANES * k : LANES * (k + 1)] = frame[k, pl.ds(z, ROWS, stride=LAYERS), :]


def partner(index, count, parity):
    other = index ^ 1 if parity == 0 else ((index - 1) ^ 1) + 1
    return other if 0 <= other < count else None


def exchange(pair, axis):
    nx, ny = lax.axis_size("gx"), lax.axis_size("gy")
    arrived = []
    for parity, value in enumerate(pair):
        moves = []
        for i in range(nx):
            for j in range(ny):
                to = (partner(i, nx, parity), j) if axis == "gx" else (i, partner(j, ny, parity))
                if None in to:
                    to = (i, j ^ 1) if axis == "gx" else (i ^ 1, j)
                moves.append((i * ny + j, to[0] * ny + to[1]))
        arrived.append(lax.ppermute(value, ("gx", "gy"), moves))
    return arrived


ANY = pl.BlockSpec(memory_space=pl.ANY)
VMEM = pl.BlockSpec(memory_space=pltpu.VMEM)


def shaped(*shape):
    return jax.ShapeDtypeStruct(shape, F32)


def call(kernel, name, ins, outs, scratch, mib, flops, moved):
    return pl.pallas_call(
        kernel,
        out_shape=outs,
        in_specs=ins,
        out_specs=jax.tree.map(lambda s: VMEM, outs),
        scratch_shapes=scratch,
        compiler_params=pltpu.CompilerParams(vmem_limit_bytes=mib << 20),
        cost_estimate=pl.CostEstimate(flops=int(flops), bytes_accessed=int(moved * (1 << 20)), transcendentals=0),
        name=name,
    )


def body(forward, adjoint, weights, density, row_edges, column_edges):
    high, low = (jnp.asarray(m) for m in cone_blocks())
    forward, adjoint, flat, weights, row_edges, column_edges = [
        pltpu.with_memory_space_constraint(x, pltpu.HBM)
        for x in (forward, adjoint, density.reshape(LAYERS * ROWS, COLS), weights, row_edges, column_edges)
    ]
    halo = shaped(2, HALO * LAYERS, LANES)
    tile = shaped(2, LAYERS * ROWS, LANES)
    whole_frame = shaped(3, FRAME_ROWS * LAYERS, LANES)
    *halo_rows, tiles = call(
        density_rows_kernel, "density_rows", [ANY], [halo, halo, tile], [pltpu.SemaphoreType.DMA((2,))], 2, 0, 1
    )(flat)
    halo_rows = exchange(halo_rows, "gx")

    side = shaped(3, SIDE * LAYERS, LANES)
    frame, *own_rows = call(
        correlate_kernel,
        "correlate",
        [ANY] * 5,
        [whole_frame, side, side],
        [
            pltpu.VMEM((2, 2, 3, 3, 2 * LAYERS, CHUNK, GROUP_COLS), BF16),
            pltpu.SMEM((2, 3), F32),
            pltpu.SMEM(row_edges.shape, jnp.int32),
            pltpu.SMEM(column_edges.shape, jnp.int32),
            pltpu.SemaphoreType.DMA((2, 2 * LAYERS)),
            pltpu.SemaphoreType.DMA((3,)),
        ],
        28,
        0,
        24,
    )(forward, adjoint, weights, row_edges, column_edges)
    own_rows = exchange(own_rows, "gx")

    column = shaped(DENSITY_PART + side_size(INNER_SIDE), LANES)
    columns = call(first_columns_kernel, "first_columns", [VMEM] * 4, [column, column], [], 2, 0, 30)(
        tiles, *halo_rows, frame
    )
    columns = exchange(columns, "gy")

    def work(count, quads, rows):
        return [
            pltpu.VMEM((count, quads * LAYERS, QUAD * PIECE), F32),
            pltpu.VMEM((count, 2, 2, rows + LAYERS * (LAGS - 2), QUAD * PIECE), BF16),
        ]

    middle_slope = call(
        slope_middle_kernel,
        "slope_middle",
        [VMEM] * 5,
        shaped(len(MIDDLE_SLOPES), SLOPE_ROWS, QUAD * PIECE),
        work(len(MIDDLE_SLOPES), DENSITY_QUADS, SLOPE_ROWS),
        12,
        1e11,
        300,
    )(tiles, *halo_rows, high, low)
    outer_slope = call(
        slope_sides_kernel,
        "slope_sides",
        [VMEM] * 7,
        shaped(2, SLOPE_ROWS, QUAD * PIECE),
        work(2, DENSITY_QUADS, SLOPE_ROWS),
        8,
        2.6e9,
        4,
    )(tiles, *halo_rows, *columns, high, low)

    own_frame = pltpu.VMEM((3, GROUP_ROWS * LAYERS, LANES), F32)
    packed = shaped(side_size(OUTER_SIDE), LANES)
    own_columns = call(columns_kernel, "columns", [VMEM] * 3, [packed, packed], [own_frame], 4, 0, 4)(frame, *own_rows)
    own_columns = exchange(own_columns, "gy")

    middle, frame = call(
        gradient_middle_kernel,
        "gradient_middle",
        [VMEM] * 8,
        [shaped(len(MIDDLE) * GRADIENT_ROWS, QUAD * PIECE), shaped(3, GROUP_ROWS * LAYERS, LANES)],
        work(len(MIDDLE), GRADIENT_QUADS, GRADIENT_ROWS),
        8,
        1e9,
        4,
    )(frame, *own_rows, *columns, middle_slope, high, low)
    return call(
        gradient_sides_kernel,
        "gradient_sides",
        [VMEM] * 8,
        shaped(*density.shape),
        [own_frame] + work(4, GRADIENT_QUADS, GRADIENT_ROWS) + [pltpu.VMEM((4 * GRADIENT_ROWS, QUAD * PIECE), F32)],
        12,
        2e9,
        4,
    )(frame, *own_columns, middle_slope, outer_slope, middle, high, low)


def solution(mesh):
    placed = (
        P(None, None, None, None, "gx", "gy"),
        P(None, None, None, None, "gx", "gy"),
        P(),
        P(None, "gx", "gy"),
        P(),
        P(),
    )
    return jax.shard_map(body, mesh=mesh, in_specs=placed, out_specs=P(None, "gx", "gy"), check_vma=False)
```

```python
import jax
import jax.numpy as jnp
import ml_dtypes
import numpy as np
from jax import lax
from jax.experimental import pallas as pl
from jax.experimental.pallas import tpu as pltpu
from jax.sharding import PartitionSpec as P

RADIUS = 10
REACH = RADIUS - 1
TAPS = 2 * REACH + 1
BETA = 64.0
ETA = 0.5
LANES = 128
LAYERS = 8
QUAD = 4
PIECE = 64
SPAN = PIECE - 2 * REACH
LAGS = 6
ROWS, COLS = 64, 256
GROUP_ROWS, GROUP_COLS = 96, 384
ROW_SLACK, COL_SLACK = 16, 64
FRAME_ROWS = GROUP_ROWS + 2 * ROW_SLACK
SIDE = ROW_SLACK + REACH
FIRST = ROW_SLACK - REACH
OWN_PART = 3 * SIDE * LAYERS
NEED = ROWS + 2 * REACH
HALO = 2 * REACH
GROUPS = LANES // HALO
GROUPED = -(-(ROWS + 2 * HALO) // GROUPS)
INNER = (SIDE + FIRST, ROWS)
HALF = (INNER[1] - INNER[0]) // 2
WINDOWS = 6
STARTS = [SPAN * w - HALO for w in range(WINDOWS)]
MIDDLE_SLOPES = (1, 2, 3, 4)
MIDDLE = (2, 3)
SLOPE_ROWS = 176
DENSITY_QUADS = SLOPE_ROWS // LAYERS + LAGS - 1
GRADIENT_ROWS = ROWS // QUAD * LAYERS
GRADIENT_QUADS = ROWS // QUAD + LAGS - 1
CHUNK = GROUP_ROWS // 3
F32 = jnp.float32
BF16 = jnp.bfloat16


def cone_blocks():
    offsets = np.arange(-RADIUS, RADIUS + 1).astype(np.float64)
    cone = np.maximum(1.0 - np.sqrt(offsets[:, None] ** 2 + offsets[None, :] ** 2) / RADIUS, 0.0)
    cone = (cone / cone.sum())[1:-1, 1:-1]
    blocks = np.zeros((LAGS, QUAD, PIECE, QUAD, PIECE))
    lanes = np.arange(2 * REACH, PIECE)
    for lag in range(LAGS):
        for source in range(QUAD):
            for target in range(QUAD):
                a = QUAD * lag + source - target
                if 0 <= a < TAPS:
                    for b in range(TAPS):
                        blocks[lag, source, lanes + b - 2 * REACH, target, lanes] = cone[a, b]
    blocks = blocks.reshape(LAGS * QUAD * PIECE, QUAD * PIECE)
    high = blocks.astype(ml_dtypes.bfloat16)
    low = (blocks - high.astype(np.float64)).astype(ml_dtypes.bfloat16)
    return high, low


def lane_of(rows):
    return lax.broadcasted_iota(jnp.int32, (rows, LANES), 1)


def turn(value, shift):
    return pltpu.roll(value, shift % LANES, 1)


def place():
    i, j = lax.axis_index("gx"), lax.axis_index("gy")
    return i, j, lax.rem(i, 2), lax.rem(j, 2)


def sides_of():
    i, j = lax.axis_index("gx"), lax.axis_index("gy")
    return i > 0, i < lax.axis_size("gx") - 1, j > 0, j < lax.axis_size("gy") - 1


def chosen(parity, first, second):
    return jnp.where(parity == 0, first, second)


def row_at(e):
    return slice(e * LAYERS, (e + 1) * LAYERS)


def half_at(e):
    return row_at(e // QUAD), slice((e % QUAD) * PIECE, (e % QUAD) * PIECE + LANES)


def piece_of(tiles, start):
    k, first = divmod(start, LANES)
    value = tiles[k]
    if first > LANES - PIECE:
        value = jnp.where(lane_of(LAYERS) >= first, value, tiles[k + 1])
    return turn(value, -first), turn(value, PIECE - first)


def correlate_part(part, forward, adjoint, weights, rows, cols, frame, out, fields, w_smem, r_smem, c_smem, sems, small):
    i, j, pi, pj = place()
    chunks = 2 - part
    base = CHUNK * (pi if part == 0 else 2 - 2 * pi)
    scalars = [
        pltpu.make_async_copy(source, target, small.at[n])
        for n, (source, target) in enumerate(((weights, w_smem), (rows, r_smem), (cols, c_smem)))
    ]

    def top_of(n):
        return pl.multiple_of(base + (lax.rem(n, 2) * CHUNK if chunks == 2 else 0), CHUNK)

    def copies(n):
        return [
            pltpu.make_async_copy(
                source.at[:, :, :, lax.div(n, chunks), pl.ds(top_of(n), CHUNK)], fields.at[k, :, :, :, n], sems.at[k, n]
            )
            for k, source in enumerate((forward, adjoint))
        ]

    for copy in scalars:
        copy.start()
    for n in range(chunks * LAYERS):
        for copy in copies(jnp.int32(n)):
            copy.start()
    yield
    for copy in scalars:
        copy.wait()
    down = r_smem[i] - i * ROWS + ROW_SLACK
    across = c_smem[j] - j * COLS + COL_SLACK
    span_rows = r_smem[i + 1] - r_smem[i]
    span_cols = c_smem[j + 1] - c_smem[j]
    lane = lane_of(16)
    row = lax.broadcasted_iota(jnp.int32, (16, LANES), 0)
    turned = lax.rem(across, LANES)

    @pl.loop(0, chunks * LAYERS)
    def _(n):
        for copy in copies(n):
            copy.wait()
        z, top = lax.div(n, chunks), top_of(n)
        for r in range(0, CHUNK, 16):
            before = jnp.zeros((16, LANES), F32)
            for k in range(3):
                at = (n, slice(r, r + 16), slice(LANES * k, LANES * (k + 1)))
                total = None
                for w in range(3):
                    real = imag = None
                    for c in range(3):
                        fr = fields[(0, 0, w, c) + at].astype(F32)
                        fi = fields[(0, 1, w, c) + at].astype(F32)
                        ar = fields[(1, 0, w, c) + at].astype(F32)
                        ai = fields[(1, 1, w, c) + at].astype(F32)
                        re = fr * ar - fi * ai
                        im = fr * ai + fi * ar
                        real = re if real is None else real + re
                        imag = im if imag is None else imag + im
                    term = w_smem[0, w] * real - w_smem[1, w] * imag
                    total = term if total is None else total + term
                inside = (row < span_rows - top - r) & (lane < span_cols - LANES * k)
                total = pltpu.roll(jnp.where(inside, total, 0.0), turned, 1)
                value = jnp.where(lane >= across, total, before)
                before = total
                frame[k, pl.ds((top + r + down) * LAYERS + z, 16, stride=LAYERS), :] = value

    start = pl.multiple_of(jnp.where(pi == 1 - part, ROWS + FIRST, 0) * LAYERS, 8)
    for k in range(3):
        out[k * SIDE * LAYERS : (k + 1) * SIDE * LAYERS, :] = frame[k, pl.ds(start, SIDE * LAYERS), :]
    yield


def correlate_first_kernel(forward, adjoint, weights, rows, cols, flat, frame, odd, even, tiles, arriving, *scratch):
    i, j, pi, pj = place()
    copies = [
        pltpu.make_async_copy(flat.at[:, LANES * k : LANES * (k + 1)], tiles.at[k], arriving.at[k]) for k in range(2)
    ]
    work = correlate_part(0, forward, adjoint, weights, rows, cols, frame, odd, *scratch)
    next(work)
    for copy in copies:
        copy.start()
    frame[...] = jnp.zeros_like(frame)
    next(work)
    for copy in copies:
        copy.wait()
    for parity in range(2):
        start = jnp.where(pi == parity, ROWS - HALO, 0)
        for r in range(HALO):
            for k in range(2):
                value = tiles[k, pl.ds(start + r, LAYERS, stride=ROWS), :]
                if parity == 0:
                    even[k, row_at(r), :] = value
                else:
                    odd[OWN_PART + (k * HALO + r) * LAYERS : OWN_PART + (k * HALO + r + 1) * LAYERS, :] = value


def correlate_second_kernel(forward, adjoint, weights, rows, cols, given, frame, out, *scratch):
    work = correlate_part(1, forward, adjoint, weights, rows, cols, frame, out, *scratch)
    next(work)
    frame[...] = given[...]
    next(work)


def density_row(tiles, even, odd, e, k):
    i, j, pi, pj = place()
    has_up, has_down, has_left, has_right = sides_of()
    if e >= ROWS + 2 * HALO:
        return jnp.zeros((LAYERS, LANES), F32)
    if HALO <= e < HALO + ROWS:
        return tiles[k, pl.ds(e - HALO, LAYERS, stride=ROWS), :]
    r = e % (HALO + ROWS)
    near, start = even[k, row_at(r), :], OWN_PART + (k * HALO + r) * LAYERS
    far = odd[start : start + LAYERS, :]
    if e < HALO:
        return jnp.where(has_up, chosen(pi, far, near), 0.0)
    return jnp.where(has_down, chosen(pi, near, far), 0.0)


def side_pack(frame, out, first_row, right, blocks, nines, count):
    tile = jnp.where(right, 2, 0)
    size = blocks[0][1] * LAYERS
    upper = lane_of(size)
    first, second = [frame[tile, at * LAYERS : at * LAYERS + size, :] for at, _ in blocks]
    swing = jnp.where(right, 0, 64)
    out[first_row : first_row + size, :] = jnp.where(
        upper >= 64, pltpu.roll(first, swing, 1), pltpu.roll(second, 64 - swing, 1)
    )
    lower = lane_of(count * LAYERS)
    packed = None
    base = jnp.where(right, LANES - 55, 64)
    for g, (at, _) in enumerate(nines):
        value = frame[tile, at * LAYERS : (at + count) * LAYERS, :]
        value = pltpu.roll(value, lax.rem(base + REACH * g, LANES), 1)
        packed = value if g == 0 else jnp.where(lower >= REACH * g, value, packed)
    out[first_row + size : first_row + size + count * LAYERS, :] = packed


def side_unpack(frame, packed, first_row, tile, valid, blocks, nines, count):
    from_left = tile == 0
    size = blocks[0][1] * LAYERS
    lane = lane_of(size)
    keep = ((lane >= 64) if from_left else (lane < 64)) & valid
    value = packed(first_row, size)
    for h, (at, _) in enumerate(blocks):
        shown = turn(value, 64) if (h == 0) != from_left else value
        frame[tile, at * LAYERS : at * LAYERS + size, :] += jnp.where(keep, shown, 0.0)
    value = packed(first_row + size, count * LAYERS)
    start = 55 if from_left else 64
    lane = lane_of(count * LAYERS)
    keep = (lane >= start) & (lane < start + REACH) & valid
    for g, (at, rows) in enumerate(nines):
        shown = jnp.where(keep, turn(value, start - REACH * g), 0.0)
        frame[tile, at * LAYERS : (at + rows) * LAYERS, :] += shown[0 : rows * LAYERS, :]


def split_rows(first, end, count):
    return [(at, min(count, end - at)) for at in range(first, end, count)]


INNER_SIDE = (((INNER[0], HALF), (INNER[0] + HALF, HALF)), split_rows(*INNER, 3), 3)
OUTER_SIDE = (((FIRST, SIDE), (ROWS, SIDE)), split_rows(FIRST, FIRST + SIDE, 4) + split_rows(ROWS, ROWS + SIDE, 4), 4)
DENSITY_PART = GROUPED * LAYERS


def side_size(side):
    return (side[0][0][1] + side[2]) * LAYERS


def first_columns_kernel(tiles, xe, xo, own, ye, yo):
    i, j, pi, pj = place()
    lane = lane_of(LAYERS)
    for r in range(GROUPED):
        left = right = None
        for g in range(GROUPS):
            a = turn(density_row(tiles, xe, xo, g * GROUPED + r, 0), HALO * g)
            b = turn(density_row(tiles, xe, xo, g * GROUPED + r, 1), HALO * g + HALO)
            left = a if g == 0 else jnp.where(lane >= HALO * g, a, left)
            right = b if g == 0 else jnp.where(lane >= HALO * g, b, right)
        ye[row_at(r), :] = chosen(pj, right, left)
        yo[row_at(r), :] = chosen(pj, left, right)
    for parity, out in ((0, ye), (1, yo)):
        side_pack(own, out, DENSITY_PART, pj == parity, *INNER_SIDE)


def banded(windows, copies, count, rows, high_ref, low_ref):
    if count > 1:
        parts = [banded(windows.at[w : w + 1], copies.at[w : w + 1], 1, rows, high_ref, low_ref) for w in range(count)]
        return jnp.concatenate(parts, axis=0)
    size = rows + LAYERS * (LAGS - 2)
    for w in range(count):
        for shift in range(2):
            for r in range(0, size, 16):
                value = windows[w, r + shift * LAYERS : r + shift * LAYERS + 16, :]
                high = value.astype(BF16)
                copies[w, shift, 0, r : r + 16, :] = high
                copies[w, shift, 1, r : r + 16, :] = (value - high.astype(F32)).astype(BF16)

    def part(kind):
        return jnp.concatenate(
            [
                jnp.concatenate(
                    [copies[w, lag % 2, kind, 16 * (lag // 2) : 16 * (lag // 2) + rows, :] for lag in range(LAGS)],
                    axis=1,
                )
                for w in range(count)
            ],
            axis=0,
        )

    high = part(0)
    out = jnp.dot(part(1), high_ref[...], preferred_element_type=F32)
    out += jnp.dot(high, low_ref[...], preferred_element_type=F32)
    return out + jnp.dot(high, high_ref[...], preferred_element_type=F32)


def slope_of(filtered):
    e = jnp.exp(-2.0 * BETA * jnp.abs(filtered - ETA))
    scale = 4.0 * BETA / (np.tanh(BETA * ETA) + np.tanh(BETA * (1.0 - ETA)))
    return np.float32(scale) * e / ((1.0 + e) * (1.0 + e))


def store_slope(value, out, count):
    for w in range(count):
        out[w] = slope_of(value[w * SLOPE_ROWS : (w + 1) * SLOPE_ROWS, :])


def slope_middle_kernel(tiles, xe, xo, high_ref, low_ref, slope, windows, copies):
    lower = lane_of(LAYERS) < PIECE
    for e in range(0, QUAD * DENSITY_QUADS, 2):
        even, odd = [[density_row(tiles, xe, xo, e + h, k) for k in range(2)] for h in range(2)]
        for n, w in enumerate(MIDDLE_SLOPES):
            windows[(n,) + half_at(e)] = jnp.where(
                lower, piece_of(even, STARTS[w])[0], piece_of(odd, STARTS[w])[1]
            )
    count = len(MIDDLE_SLOPES)
    store_slope(banded(windows, copies, count, SLOPE_ROWS, high_ref, low_ref), slope, count)


def slope_sides_kernel(tiles, xe, xo, ye, yo, high_ref, low_ref, slope, windows, copies):
    i, j, pi, pj = place()
    has_up, has_down, has_left, has_right = sides_of()
    lane = lane_of(LAYERS)
    lower = lane < PIECE
    within = jnp.where(lower, lane, lane - PIECE)
    own_left, own_right = within >= HALO, within < COLS - STARTS[-1]
    edge = within < COLS - STARTS[-1] + HALO
    for e in range(0, QUAD * DENSITY_QUADS, 2):
        lefts, rights = [], []
        for h in range(2):
            g, r = divmod(min(e + h, GROUPS * GROUPED - 1), GROUPED)
            at = row_at(r)
            left = jnp.where(has_left, chosen(pj, yo[at, :], ye[at, :]), 0.0)
            right = jnp.where(has_right, chosen(pj, ye[at, :], yo[at, :]), 0.0)
            left = turn(left, PIECE * h - HALO * g)
            right = turn(right, PIECE * h + COLS - STARTS[-1] - HALO * g)
            t0, t1 = [density_row(tiles, xe, xo, e + h, k) for k in range(2)]
            lefts.append(jnp.where(own_left, turn(t0, PIECE * h - STARTS[0]), left))
            rights.append(
                jnp.where(own_right, turn(t1, PIECE * h + LANES - STARTS[-1]), jnp.where(edge, right, 0.0))
            )
        windows[(0,) + half_at(e)] = jnp.where(lower, *lefts)
        windows[(1,) + half_at(e)] = jnp.where(lower, *rights)
    store_slope(banded(windows, copies, 2, SLOPE_ROWS, high_ref, low_ref), slope, 2)


def add_rows(frame, xe, xo, tiles):
    i, j, pi, pj = place()
    has_up, has_down, has_left, has_right = sides_of()
    size = SIDE * LAYERS
    for k in tiles:
        near, far = [ref[k * size : (k + 1) * size, :] for ref in (xe, xo)]
        frame[k, FIRST * LAYERS : FIRST * LAYERS + size, :] += jnp.where(has_up, chosen(pi, far, near), 0.0)
        frame[k, ROWS * LAYERS : ROWS * LAYERS + size, :] += jnp.where(has_down, chosen(pi, near, far), 0.0)


def columns_kernel(own, xe, xo, ye, yo, frame):
    i, j, pi, pj = place()
    for k in (0, 2):
        frame[k] = own[k, 0 : GROUP_ROWS * LAYERS, :]
    add_rows(frame, xe, xo, (0, 2))
    for parity, out in ((0, ye), (1, yo)):
        side_pack(frame, out, 0, pj == parity, *OUTER_SIDE)


def add_columns(frame, ye, yo, first_row, side):
    i, j, pi, pj = place()
    has_up, has_down, has_left, has_right = sides_of()

    def pick(first, second):
        return lambda at, count: chosen(pj, first[at : at + count, :], second[at : at + count, :])

    side_unpack(frame, pick(yo, ye), first_row, 0, has_left, *side)
    side_unpack(frame, pick(ye, yo), first_row, 2, has_right, *side)


def weigh(frame, windows, n, w, slope, before):
    lane = lane_of(LAYERS)
    lower = lane < PIECE
    own = jnp.where(lower, lane, lane - PIECE) >= 2 * REACH
    for e in range(0, QUAD * GRADIENT_QUADS, 2):
        at = half_at(e)
        even, odd = [[frame[k, row_at(FIRST + e + h), :] for k in range(3)] for h in range(2)]
        start = STARTS[w] - REACH + COL_SLACK
        factor = slope[at] if before is None else jnp.where(own, slope[at], turn(before[at], -SPAN))
        windows[(n,) + at] = jnp.where(lower, piece_of(even, start)[0], piece_of(odd, start)[1]) * factor


def gradient_middle_kernel(own, xe, xo, ye, yo, slope, high_ref, low_ref, out, frame, windows, copies):
    frame[...] = own[:, 0 : GROUP_ROWS * LAYERS, :]
    add_rows(frame, xe, xo, range(3))
    for n, w in enumerate(MIDDLE):
        weigh(frame, windows, n, w, slope.at[w - 1], slope.at[w - 2])
    out[...] = banded(windows, copies, len(MIDDLE), GRADIENT_ROWS, high_ref, low_ref)
    add_columns(frame, ye, yo, DENSITY_PART, INNER_SIDE)


def gradient_sides_kernel(given, ye, yo, slope, outer, middle, high_ref, low_ref, out, frame, windows, copies, result):
    frame[...] = given[...]
    add_columns(frame, ye, yo, 0, OUTER_SIDE)
    weigh(frame, windows, 0, 0, outer.at[0], None)
    weigh(frame, windows, 1, 1, slope.at[0], outer.at[0])
    weigh(frame, windows, 2, 4, slope.at[3], slope.at[2])
    weigh(frame, windows, 3, 5, outer.at[1], slope.at[3])
    result[...] = banded(windows, copies, 4, GRADIENT_ROWS, high_ref, low_ref)
    lane = lane_of(LAYERS)
    places = ((result, 0), (result, 1), (middle, 0), (middle, 1), (result, 2), (result, 3))
    for e in range(ROWS):
        rows, lanes = half_at(e - e % 2)
        pieces = []
        for w, (source, n) in enumerate(places):
            at = slice(rows.start + n * GRADIENT_ROWS, rows.stop + n * GRADIENT_ROWS)
            pieces.append(turn(source[at, lanes], STARTS[w] - 2 * REACH - PIECE * (e % 2)))
        for k in range(2):
            value = None
            for w, piece in enumerate(pieces):
                first = STARTS[w] - LANES * k
                if first < LANES and first + SPAN > 0:
                    value = piece if value is None else jnp.where(lane >= first, piece, value)
            frame[k, row_at(e), :] = value
    for z in range(LAYERS):
        for k in range(2):
            out[z, :, LANES * k : LANES * (k + 1)] = frame[k, pl.ds(z, ROWS, stride=LAYERS), :]


def partner(index, count, parity):
    other = index ^ 1 if parity == 0 else ((index - 1) ^ 1) + 1
    return other if 0 <= other < count else None


def exchange(value, axis, parity):
    nx, ny = lax.axis_size("gx"), lax.axis_size("gy")
    moves = []
    for i in range(nx):
        for j in range(ny):
            to = (partner(i, nx, parity), j) if axis == "gx" else (i, partner(j, ny, parity))
            if None in to:
                to = (i, j ^ 1) if axis == "gx" else (i ^ 1, j)
            moves.append((i * ny + j, to[0] * ny + to[1]))
    return lax.ppermute(value, ("gx", "gy"), moves)


def exchange_both(pair, axis):
    return [exchange(value, axis, parity) for parity, value in enumerate(pair)]


ANY = pl.BlockSpec(memory_space=pl.ANY)
VMEM = pl.BlockSpec(memory_space=pltpu.VMEM)


def shaped(*shape):
    return jax.ShapeDtypeStruct(shape, F32)


def call(kernel, name, ins, outs, scratch, mib, flops, moved):
    return pl.pallas_call(
        kernel,
        out_shape=outs,
        in_specs=ins,
        out_specs=jax.tree.map(lambda s: VMEM, outs),
        scratch_shapes=scratch,
        compiler_params=pltpu.CompilerParams(vmem_limit_bytes=mib << 20),
        cost_estimate=pl.CostEstimate(flops=int(flops), bytes_accessed=int(moved * (1 << 20)), transcendentals=0),
        name=name,
    )


def body(forward, adjoint, weights, density, row_edges, column_edges):
    high, low = (jnp.asarray(m) for m in cone_blocks())
    forward, adjoint, flat, weights, row_edges, column_edges = [
        pltpu.with_memory_space_constraint(x, pltpu.HBM)
        for x in (forward, adjoint, density.reshape(LAYERS * ROWS, COLS), weights, row_edges, column_edges)
    ]
    halo = shaped(2, HALO * LAYERS, LANES)
    tile = shaped(2, LAYERS * ROWS, LANES)
    whole_frame = shaped(3, FRAME_ROWS * LAYERS, LANES)
    def correlate(kernel, name, chunks, ins, outs, scratch, mib):
        return call(
            kernel,
            name,
            ins,
            [whole_frame] + outs,
            scratch
            + [
                pltpu.VMEM((2, 2, 3, 3, chunks * LAYERS, CHUNK, GROUP_COLS), BF16),
                pltpu.SMEM((2, 3), F32),
                pltpu.SMEM(row_edges.shape, jnp.int32),
                pltpu.SMEM(column_edges.shape, jnp.int32),
                pltpu.SemaphoreType.DMA((2, chunks * LAYERS)),
                pltpu.SemaphoreType.DMA((3,)),
            ],
            mib,
            0,
            8 * chunks,
        )

    given = (forward, adjoint, weights, row_edges, column_edges)
    frame, odd, even, tiles = correlate(
        correlate_first_kernel,
        "correlate_first",
        2,
        [ANY] * 6,
        [shaped(OWN_PART + 2 * HALO * LAYERS, LANES), halo, tile],
        [pltpu.SemaphoreType.DMA((2,))],
        20,
    )(*given, flat)
    odd = exchange(odd, "gx", 1)
    halo_rows = [exchange(even, "gx", 0), odd]
    frame, own_even = correlate(
        correlate_second_kernel, "correlate_second", 1, [ANY] * 5 + [VMEM], [shaped(OWN_PART, LANES)], [], 14
    )(*given, frame)
    own_rows = [exchange(own_even, "gx", 0), odd]

    column = shaped(DENSITY_PART + side_size(INNER_SIDE), LANES)
    columns = call(first_columns_kernel, "first_columns", [VMEM] * 4, [column, column], [], 2, 0, 30)(
        tiles, *halo_rows, frame
    )
    columns = exchange_both(columns, "gy")

    def work(count, quads, rows):
        return [
            pltpu.VMEM((count, quads * LAYERS, QUAD * PIECE), F32),
            pltpu.VMEM((count, 2, 2, rows + LAYERS * (LAGS - 2), QUAD * PIECE), BF16),
        ]

    middle_slope = call(
        slope_middle_kernel,
        "slope_middle",
        [VMEM] * 5,
        shaped(len(MIDDLE_SLOPES), SLOPE_ROWS, QUAD * PIECE),
        work(len(MIDDLE_SLOPES), DENSITY_QUADS, SLOPE_ROWS),
        12,
        1e11,
        300,
    )(tiles, *halo_rows, high, low)
    outer_slope = call(
        slope_sides_kernel,
        "slope_sides",
        [VMEM] * 7,
        shaped(2, SLOPE_ROWS, QUAD * PIECE),
        work(2, DENSITY_QUADS, SLOPE_ROWS),
        8,
        2.6e9,
        4,
    )(tiles, *halo_rows, *columns, high, low)

    own_frame = pltpu.VMEM((3, GROUP_ROWS * LAYERS, LANES), F32)
    packed = shaped(side_size(OUTER_SIDE), LANES)
    own_columns = call(columns_kernel, "columns", [VMEM] * 3, [packed, packed], [own_frame], 4, 0, 4)(frame, *own_rows)
    own_columns = exchange_both(own_columns, "gy")

    middle, frame = call(
        gradient_middle_kernel,
        "gradient_middle",
        [VMEM] * 8,
        [shaped(len(MIDDLE) * GRADIENT_ROWS, QUAD * PIECE), shaped(3, GROUP_ROWS * LAYERS, LANES)],
        work(len(MIDDLE), GRADIENT_QUADS, GRADIENT_ROWS),
        8,
        1e9,
        4,
    )(frame, *own_rows, *columns, middle_slope, high, low)
    return call(
        gradient_sides_kernel,
        "gradient_sides",
        [VMEM] * 8,
        shaped(*density.shape),
        [own_frame] + work(4, GRADIENT_QUADS, GRADIENT_ROWS) + [pltpu.VMEM((4 * GRADIENT_ROWS, QUAD * PIECE), F32)],
        12,
        2e9,
        4,
    )(frame, *own_columns, middle_slope, outer_slope, middle, high, low)


def solution(mesh):
    placed = (
        P(None, None, None, None, "gx", "gy"),
        P(None, None, None, None, "gx", "gy"),
        P(),
        P(None, "gx", "gy"),
        P(),
        P(),
    )
    return jax.shard_map(body, mesh=mesh, in_specs=placed, out_specs=P(None, "gx", "gy"), check_vma=False)
```

```python
import jax
import jax.numpy as jnp
import ml_dtypes
import numpy as np
from jax import lax
from jax.experimental import pallas as pl
from jax.experimental.pallas import tpu as pltpu
from jax.sharding import PartitionSpec as P

RADIUS = 10
REACH = RADIUS - 1
TAPS = 2 * REACH + 1
BETA = 64.0
ETA = 0.5
LANES = 128
LAYERS = 8
QUAD = 4
PIECE = 64
SPAN = PIECE - 2 * REACH
LAGS = 6
ROWS, COLS = 64, 256
GROUP_ROWS, GROUP_COLS = 96, 384
ROW_SLACK, COL_SLACK = 16, 64
FRAME_ROWS = GROUP_ROWS + 2 * ROW_SLACK
SIDE = ROW_SLACK + REACH
FIRST = ROW_SLACK - REACH
OWN_PART = 3 * SIDE * LAYERS
NEED = ROWS + 2 * REACH
HALO = 2 * REACH
GROUPS = LANES // HALO
GROUPED = -(-(ROWS + 2 * HALO) // GROUPS)
INNER = (SIDE + FIRST, ROWS)
HALF = (INNER[1] - INNER[0]) // 2
WINDOWS = 6
STARTS = [SPAN * w - HALO for w in range(WINDOWS)]
MIDDLE_SLOPES = (1, 2, 3, 4)
MIDDLE = (2, 3)
SLOPE_ROWS = 176
DENSITY_QUADS = SLOPE_ROWS // LAYERS + LAGS - 1
GRADIENT_ROWS = ROWS // QUAD * LAYERS
GRADIENT_QUADS = ROWS // QUAD + LAGS - 1
CHUNK = GROUP_ROWS // 3
F32 = jnp.float32
BF16 = jnp.bfloat16


def cone_blocks():
    offsets = np.arange(-RADIUS, RADIUS + 1).astype(np.float64)
    cone = np.maximum(1.0 - np.sqrt(offsets[:, None] ** 2 + offsets[None, :] ** 2) / RADIUS, 0.0)
    cone = (cone / cone.sum())[1:-1, 1:-1]
    blocks = np.zeros((LAGS, QUAD, PIECE, QUAD, PIECE))
    lanes = np.arange(2 * REACH, PIECE)
    for lag in range(LAGS):
        for source in range(QUAD):
            for target in range(QUAD):
                a = QUAD * lag + source - target
                if 0 <= a < TAPS:
                    for b in range(TAPS):
                        blocks[lag, source, lanes + b - 2 * REACH, target, lanes] = cone[a, b]
    blocks = blocks.reshape(LAGS * QUAD * PIECE, QUAD * PIECE)
    high = blocks.astype(ml_dtypes.bfloat16)
    low = (blocks - high.astype(np.float64)).astype(ml_dtypes.bfloat16)
    return high, low


def lane_of(rows):
    return lax.broadcasted_iota(jnp.int32, (rows, LANES), 1)


def turn(value, shift):
    return pltpu.roll(value, shift % LANES, 1)


def place():
    i, j = lax.axis_index("gx"), lax.axis_index("gy")
    return i, j, lax.rem(i, 2), lax.rem(j, 2)


def sides_of():
    i, j = lax.axis_index("gx"), lax.axis_index("gy")
    return i > 0, i < lax.axis_size("gx") - 1, j > 0, j < lax.axis_size("gy") - 1


def chosen(parity, first, second):
    return jnp.where(parity == 0, first, second)


def row_at(e):
    return slice(e * LAYERS, (e + 1) * LAYERS)


def half_at(e):
    return row_at(e // QUAD), slice((e % QUAD) * PIECE, (e % QUAD) * PIECE + LANES)


def piece_of(tiles, start):
    k, first = divmod(start, LANES)
    value = tiles[k]
    if first > LANES - PIECE:
        value = jnp.where(lane_of(LAYERS) >= first, value, tiles[k + 1])
    return turn(value, -first), turn(value, PIECE - first)


def correlate_part(part, forward, adjoint, weights, rows, cols, frame, out, fields, w_smem, r_smem, c_smem, sems, small):
    i, j, pi, pj = place()
    chunks = 2 - part
    base = CHUNK * (pi if part == 0 else 2 - 2 * pi)
    scalars = [
        pltpu.make_async_copy(source, target, small.at[n])
        for n, (source, target) in enumerate(((weights, w_smem), (rows, r_smem), (cols, c_smem)))
    ]

    def top_of(n):
        return pl.multiple_of(base + (lax.rem(n, 2) * CHUNK if chunks == 2 else 0), CHUNK)

    def copies(n):
        return [
            pltpu.make_async_copy(
                source.at[:, :, :, lax.div(n, chunks), pl.ds(top_of(n), CHUNK)], fields.at[k, :, :, :, n], sems.at[k, n]
            )
            for k, source in enumerate((forward, adjoint))
        ]

    for copy in scalars:
        copy.start()
    for n in range(chunks * LAYERS):
        for copy in copies(jnp.int32(n)):
            copy.start()
    yield
    for copy in scalars:
        copy.wait()
    down = r_smem[i] - i * ROWS + ROW_SLACK
    across = c_smem[j] - j * COLS + COL_SLACK
    span_rows = r_smem[i + 1] - r_smem[i]
    span_cols = c_smem[j + 1] - c_smem[j]
    lane = lane_of(16)
    row = lax.broadcasted_iota(jnp.int32, (16, LANES), 0)
    turned = lax.rem(across, LANES)

    @pl.loop(0, chunks * LAYERS)
    def _(n):
        for copy in copies(n):
            copy.wait()
        z, top = lax.div(n, chunks), top_of(n)
        for r in range(0, CHUNK, 16):
            before = jnp.zeros((16, LANES), F32)
            for k in range(3):
                at = (n, slice(r, r + 16), slice(LANES * k, LANES * (k + 1)))
                total = None
                for w in range(3):
                    real = imag = None
                    for c in range(3):
                        fr = fields[(0, 0, w, c) + at].astype(F32)
                        fi = fields[(0, 1, w, c) + at].astype(F32)
                        ar = fields[(1, 0, w, c) + at].astype(F32)
                        ai = fields[(1, 1, w, c) + at].astype(F32)
                        re = fr * ar - fi * ai
                        im = fr * ai + fi * ar
                        real = re if real is None else real + re
                        imag = im if imag is None else imag + im
                    term = w_smem[0, w] * real - w_smem[1, w] * imag
                    total = term if total is None else total + term
                inside = (row < span_rows - top - r) & (lane < span_cols - LANES * k)
                total = pltpu.roll(jnp.where(inside, total, 0.0), turned, 1)
                value = jnp.where(lane >= across, total, before)
                before = total
                frame[k, pl.ds((top + r + down) * LAYERS + z, 16, stride=LAYERS), :] = value

    start = pl.multiple_of(jnp.where(pi == 1 - part, ROWS + FIRST, 0) * LAYERS, 8)
    for k in range(3):
        out[k * SIDE * LAYERS : (k + 1) * SIDE * LAYERS, :] = frame[k, pl.ds(start, SIDE * LAYERS), :]
    yield


def correlate_first_kernel(forward, adjoint, weights, rows, cols, flat, frame, odd, even, tiles, arriving, *scratch):
    i, j, pi, pj = place()
    copies = [
        pltpu.make_async_copy(flat.at[:, LANES * k : LANES * (k + 1)], tiles.at[k], arriving.at[k]) for k in range(2)
    ]
    work = correlate_part(0, forward, adjoint, weights, rows, cols, frame, odd, *scratch)
    next(work)
    for copy in copies:
        copy.start()
    frame[...] = jnp.zeros_like(frame)
    next(work)
    for copy in copies:
        copy.wait()
    for parity in range(2):
        start = jnp.where(pi == parity, ROWS - HALO, 0)
        for r in range(HALO):
            for k in range(2):
                value = tiles[k, pl.ds(start + r, LAYERS, stride=ROWS), :]
                if parity == 0:
                    even[k, row_at(r), :] = value
                else:
                    odd[OWN_PART + (k * HALO + r) * LAYERS : OWN_PART + (k * HALO + r + 1) * LAYERS, :] = value


def correlate_second_kernel(forward, adjoint, weights, rows, cols, given, frame, out, *scratch):
    work = correlate_part(1, forward, adjoint, weights, rows, cols, frame, out, *scratch)
    next(work)
    frame[...] = given[...]
    next(work)


def density_row(tiles, even, odd, e, k):
    i, j, pi, pj = place()
    has_up, has_down, has_left, has_right = sides_of()
    if e >= ROWS + 2 * HALO:
        return jnp.zeros((LAYERS, LANES), F32)
    if HALO <= e < HALO + ROWS:
        return tiles[k, pl.ds(e - HALO, LAYERS, stride=ROWS), :]
    r = e % (HALO + ROWS)
    near, start = even[k, row_at(r), :], OWN_PART + (k * HALO + r) * LAYERS
    far = odd[start : start + LAYERS, :]
    if e < HALO:
        return jnp.where(has_up, chosen(pi, far, near), 0.0)
    return jnp.where(has_down, chosen(pi, near, far), 0.0)


def side_pack(frame, out, first_row, right, blocks, nines, count):
    tile = jnp.where(right, 2, 0)
    size = blocks[0][1] * LAYERS
    upper = lane_of(size)
    first, second = [frame[tile, at * LAYERS : at * LAYERS + size, :] for at, _ in blocks]
    swing = jnp.where(right, 0, 64)
    out[first_row : first_row + size, :] = jnp.where(
        upper >= 64, pltpu.roll(first, swing, 1), pltpu.roll(second, 64 - swing, 1)
    )
    lower = lane_of(count * LAYERS)
    packed = None
    base = jnp.where(right, LANES - 55, 64)
    for g, (at, _) in enumerate(nines):
        value = frame[tile, at * LAYERS : (at + count) * LAYERS, :]
        value = pltpu.roll(value, lax.rem(base + REACH * g, LANES), 1)
        packed = value if g == 0 else jnp.where(lower >= REACH * g, value, packed)
    out[first_row + size : first_row + size + count * LAYERS, :] = packed


def side_unpack(frame, packed, first_row, tile, valid, blocks, nines, count):
    from_left = tile == 0
    size = blocks[0][1] * LAYERS
    lane = lane_of(size)
    keep = ((lane >= 64) if from_left else (lane < 64)) & valid
    value = packed(first_row, size)
    for h, (at, _) in enumerate(blocks):
        shown = turn(value, 64) if (h == 0) != from_left else value
        frame[tile, at * LAYERS : at * LAYERS + size, :] += jnp.where(keep, shown, 0.0)
    value = packed(first_row + size, count * LAYERS)
    start = 55 if from_left else 64
    lane = lane_of(count * LAYERS)
    keep = (lane >= start) & (lane < start + REACH) & valid
    for g, (at, rows) in enumerate(nines):
        shown = jnp.where(keep, turn(value, start - REACH * g), 0.0)
        frame[tile, at * LAYERS : (at + rows) * LAYERS, :] += shown[0 : rows * LAYERS, :]


def split_rows(first, end, count):
    return [(at, min(count, end - at)) for at in range(first, end, count)]


INNER_SIDE = (((INNER[0], HALF), (INNER[0] + HALF, HALF)), split_rows(*INNER, 3), 3)
OUTER_SIDE = (((FIRST, SIDE), (ROWS, SIDE)), split_rows(FIRST, FIRST + SIDE, 4) + split_rows(ROWS, ROWS + SIDE, 4), 4)
DENSITY_PART = GROUPED * LAYERS


def side_size(side):
    return (side[0][0][1] + side[2]) * LAYERS


def first_columns_kernel(tiles, xe, xo, own, ye, yo):
    i, j, pi, pj = place()
    lane = lane_of(LAYERS)
    for r in range(GROUPED):
        left = right = None
        for g in range(GROUPS):
            a = turn(density_row(tiles, xe, xo, g * GROUPED + r, 0), HALO * g)
            b = turn(density_row(tiles, xe, xo, g * GROUPED + r, 1), HALO * g + HALO)
            left = a if g == 0 else jnp.where(lane >= HALO * g, a, left)
            right = b if g == 0 else jnp.where(lane >= HALO * g, b, right)
        ye[row_at(r), :] = chosen(pj, right, left)
        yo[row_at(r), :] = chosen(pj, left, right)
    for parity, out in ((0, ye), (1, yo)):
        side_pack(own, out, DENSITY_PART, pj == parity, *INNER_SIDE)


def banded(windows, copies, count, rows, high_ref, low_ref):
    if count > 1:
        parts = [banded(windows.at[w : w + 1], copies.at[w : w + 1], 1, rows, high_ref, low_ref) for w in range(count)]
        return jnp.concatenate(parts, axis=0)
    size = rows + LAYERS * (LAGS - 2)
    for w in range(count):
        for shift in range(2):
            for r in range(0, size, 16):
                value = windows[w, r + shift * LAYERS : r + shift * LAYERS + 16, :]
                high = value.astype(BF16)
                copies[w, shift, 0, r : r + 16, :] = high
                copies[w, shift, 1, r : r + 16, :] = (value - high.astype(F32)).astype(BF16)

    def part(kind):
        return jnp.concatenate(
            [
                jnp.concatenate(
                    [copies[w, lag % 2, kind, 16 * (lag // 2) : 16 * (lag // 2) + rows, :] for lag in range(LAGS)],
                    axis=1,
                )
                for w in range(count)
            ],
            axis=0,
        )

    high = part(0)
    out = jnp.dot(part(1), high_ref[...], preferred_element_type=F32)
    out += jnp.dot(high, low_ref[...], preferred_element_type=F32)
    return out + jnp.dot(high, high_ref[...], preferred_element_type=F32)


def slope_of(filtered):
    e = jnp.exp(-2.0 * BETA * jnp.abs(filtered - ETA))
    scale = 4.0 * BETA / (np.tanh(BETA * ETA) + np.tanh(BETA * (1.0 - ETA)))
    return np.float32(scale) * e / ((1.0 + e) * (1.0 + e))


def store_slope(value, out, count):
    for w in range(count):
        out[w] = slope_of(value[w * SLOPE_ROWS : (w + 1) * SLOPE_ROWS, :])


def slope_middle_kernel(tiles, xe, xo, high_ref, low_ref, slope, windows, copies):
    lower = lane_of(LAYERS) < PIECE
    for e in range(0, QUAD * DENSITY_QUADS, 2):
        even, odd = [[density_row(tiles, xe, xo, e + h, k) for k in range(2)] for h in range(2)]
        for n, w in enumerate(MIDDLE_SLOPES):
            windows[(n,) + half_at(e)] = jnp.where(
                lower, piece_of(even, STARTS[w])[0], piece_of(odd, STARTS[w])[1]
            )
    count = len(MIDDLE_SLOPES)
    store_slope(banded(windows, copies, count, SLOPE_ROWS, high_ref, low_ref), slope, count)


def slope_sides_kernel(tiles, xe, xo, ye, yo, high_ref, low_ref, slope, windows, copies):
    i, j, pi, pj = place()
    has_up, has_down, has_left, has_right = sides_of()
    lane = lane_of(LAYERS)
    lower = lane < PIECE
    within = jnp.where(lower, lane, lane - PIECE)
    own_left, own_right = within >= HALO, within < COLS - STARTS[-1]
    edge = within < COLS - STARTS[-1] + HALO
    for e in range(0, QUAD * DENSITY_QUADS, 2):
        lefts, rights = [], []
        for h in range(2):
            g, r = divmod(min(e + h, GROUPS * GROUPED - 1), GROUPED)
            at = row_at(r)
            left = jnp.where(has_left, chosen(pj, yo[at, :], ye[at, :]), 0.0)
            right = jnp.where(has_right, chosen(pj, ye[at, :], yo[at, :]), 0.0)
            left = turn(left, PIECE * h - HALO * g)
            right = turn(right, PIECE * h + COLS - STARTS[-1] - HALO * g)
            t0, t1 = [density_row(tiles, xe, xo, e + h, k) for k in range(2)]
            lefts.append(jnp.where(own_left, turn(t0, PIECE * h - STARTS[0]), left))
            rights.append(
                jnp.where(own_right, turn(t1, PIECE * h + LANES - STARTS[-1]), jnp.where(edge, right, 0.0))
            )
        windows[(0,) + half_at(e)] = jnp.where(lower, *lefts)
        windows[(1,) + half_at(e)] = jnp.where(lower, *rights)
    store_slope(banded(windows, copies, 2, SLOPE_ROWS, high_ref, low_ref), slope, 2)


def add_rows(frame, xe, xo, tiles):
    i, j, pi, pj = place()
    has_up, has_down, has_left, has_right = sides_of()
    size = SIDE * LAYERS
    for k in tiles:
        near, far = [ref[k * size : (k + 1) * size, :] for ref in (xe, xo)]
        frame[k, FIRST * LAYERS : FIRST * LAYERS + size, :] += jnp.where(has_up, chosen(pi, far, near), 0.0)
        frame[k, ROWS * LAYERS : ROWS * LAYERS + size, :] += jnp.where(has_down, chosen(pi, near, far), 0.0)


def columns_kernel(own, xe, xo, ye, yo, frame):
    i, j, pi, pj = place()
    for k in (0, 2):
        frame[k] = own[k, 0 : GROUP_ROWS * LAYERS, :]
    add_rows(frame, xe, xo, (0, 2))
    for parity, out in ((0, ye), (1, yo)):
        side_pack(frame, out, 0, pj == parity, *OUTER_SIDE)


def add_columns(frame, ye, yo, first_row, side):
    i, j, pi, pj = place()
    has_up, has_down, has_left, has_right = sides_of()

    def pick(first, second):
        return lambda at, count: chosen(pj, first[at : at + count, :], second[at : at + count, :])

    side_unpack(frame, pick(yo, ye), first_row, 0, has_left, *side)
    side_unpack(frame, pick(ye, yo), first_row, 2, has_right, *side)


def weigh(tiles, windows, n, w, slope, before):
    lane = lane_of(LAYERS)
    lower = lane < PIECE
    own = jnp.where(lower, lane, lane - PIECE) >= 2 * REACH
    for e in range(0, QUAD * GRADIENT_QUADS, 2):
        at = half_at(e)
        even, odd = [[tile[row_at(FIRST + e + h), :] for tile in tiles] for h in range(2)]
        start = STARTS[w] - REACH + COL_SLACK
        factor = slope[at] if before is None else jnp.where(own, slope[at], turn(before[at], -SPAN))
        windows[(n,) + at] = jnp.where(lower, piece_of(even, start)[0], piece_of(odd, start)[1]) * factor


def gradient_middle_kernel(own, xe, xo, ye, yo, slope, high_ref, low_ref, out, frame, windows, copies):
    frame[...] = own[:, 0 : GROUP_ROWS * LAYERS, :]
    add_rows(frame, xe, xo, range(3))
    for n, w in enumerate(MIDDLE):
        weigh([frame.at[k] for k in range(3)], windows, n, w, slope.at[w - 1], slope.at[w - 2])
    out[...] = banded(windows, copies, len(MIDDLE), GRADIENT_ROWS, high_ref, low_ref)
    add_columns(frame, ye, yo, DENSITY_PART, INNER_SIDE)


def gradient_sides_kernel(given, ye, yo, slope, outer, middle, high_ref, low_ref, out, frame, windows, copies, result):
    for k in (0, 2):
        frame[k] = given[k]
    add_columns(frame, ye, yo, 0, OUTER_SIDE)
    frame_tiles = (frame.at[0], given.at[1], frame.at[2])
    weigh(frame_tiles, windows, 0, 0, outer.at[0], None)
    weigh(frame_tiles, windows, 1, 1, slope.at[0], outer.at[0])
    weigh(frame_tiles, windows, 2, 4, slope.at[3], slope.at[2])
    weigh(frame_tiles, windows, 3, 5, outer.at[1], slope.at[3])
    result[...] = banded(windows, copies, 4, GRADIENT_ROWS, high_ref, low_ref)
    lane = lane_of(LAYERS)
    places = ((result, 0), (result, 1), (middle, 0), (middle, 1), (result, 2), (result, 3))
    for e in range(ROWS):
        rows, lanes = half_at(e - e % 2)
        pieces = []
        for w, (source, n) in enumerate(places):
            at = slice(rows.start + n * GRADIENT_ROWS, rows.stop + n * GRADIENT_ROWS)
            pieces.append(turn(source[at, lanes], STARTS[w] - 2 * REACH - PIECE * (e % 2)))
        for k in range(2):
            value = None
            for w, piece in enumerate(pieces):
                first = STARTS[w] - LANES * k
                if first < LANES and first + SPAN > 0:
                    value = piece if value is None else jnp.where(lane >= first, piece, value)
            frame[k, row_at(e), :] = value
    for z in range(LAYERS):
        for k in range(2):
            out[z, :, LANES * k : LANES * (k + 1)] = frame[k, pl.ds(z, ROWS, stride=LAYERS), :]


def partner(index, count, parity):
    other = index ^ 1 if parity == 0 else ((index - 1) ^ 1) + 1
    return other if 0 <= other < count else None


def exchange(value, axis, parity):
    nx, ny = lax.axis_size("gx"), lax.axis_size("gy")
    moves = []
    for i in range(nx):
        for j in range(ny):
            to = (partner(i, nx, parity), j) if axis == "gx" else (i, partner(j, ny, parity))
            if None in to:
                to = (i, j ^ 1) if axis == "gx" else (i ^ 1, j)
            moves.append((i * ny + j, to[0] * ny + to[1]))
    return lax.ppermute(value, ("gx", "gy"), moves)


def exchange_both(pair, axis):
    return [exchange(value, axis, parity) for parity, value in enumerate(pair)]


ANY = pl.BlockSpec(memory_space=pl.ANY)
VMEM = pl.BlockSpec(memory_space=pltpu.VMEM)


def shaped(*shape):
    return jax.ShapeDtypeStruct(shape, F32)


def call(kernel, name, ins, outs, scratch, mib, flops, moved):
    return pl.pallas_call(
        kernel,
        out_shape=outs,
        in_specs=ins,
        out_specs=jax.tree.map(lambda s: VMEM, outs),
        scratch_shapes=scratch,
        compiler_params=pltpu.CompilerParams(vmem_limit_bytes=mib << 20),
        cost_estimate=pl.CostEstimate(flops=int(flops), bytes_accessed=int(moved * (1 << 20)), transcendentals=0),
        name=name,
    )


def body(forward, adjoint, weights, density, row_edges, column_edges):
    high, low = (jnp.asarray(m) for m in cone_blocks())
    forward, adjoint, flat, weights, row_edges, column_edges = [
        pltpu.with_memory_space_constraint(x, pltpu.HBM)
        for x in (forward, adjoint, density.reshape(LAYERS * ROWS, COLS), weights, row_edges, column_edges)
    ]
    halo = shaped(2, HALO * LAYERS, LANES)
    tile = shaped(2, LAYERS * ROWS, LANES)
    whole_frame = shaped(3, FRAME_ROWS * LAYERS, LANES)
    def correlate(kernel, name, chunks, ins, outs, scratch, mib):
        return call(
            kernel,
            name,
            ins,
            [whole_frame] + outs,
            scratch
            + [
                pltpu.VMEM((2, 2, 3, 3, chunks * LAYERS, CHUNK, GROUP_COLS), BF16),
                pltpu.SMEM((2, 3), F32),
                pltpu.SMEM(row_edges.shape, jnp.int32),
                pltpu.SMEM(column_edges.shape, jnp.int32),
                pltpu.SemaphoreType.DMA((2, chunks * LAYERS)),
                pltpu.SemaphoreType.DMA((3,)),
            ],
            mib,
            0,
            8 * chunks,
        )

    given = (forward, adjoint, weights, row_edges, column_edges)
    frame, odd, even, tiles = correlate(
        correlate_first_kernel,
        "correlate_first",
        2,
        [ANY] * 6,
        [shaped(OWN_PART + 2 * HALO * LAYERS, LANES), halo, tile],
        [pltpu.SemaphoreType.DMA((2,))],
        20,
    )(*given, flat)
    odd = exchange(odd, "gx", 1)
    halo_rows = [exchange(even, "gx", 0), odd]
    frame, own_even = correlate(
        correlate_second_kernel, "correlate_second", 1, [ANY] * 5 + [VMEM], [shaped(OWN_PART, LANES)], [], 14
    )(*given, frame)
    own_rows = [exchange(own_even, "gx", 0), odd]

    column = shaped(DENSITY_PART + side_size(INNER_SIDE), LANES)
    columns = call(first_columns_kernel, "first_columns", [VMEM] * 4, [column, column], [], 2, 0, 30)(
        tiles, *halo_rows, frame
    )
    columns = exchange_both(columns, "gy")

    def work(count, quads, rows):
        return [
            pltpu.VMEM((count, quads * LAYERS, QUAD * PIECE), F32),
            pltpu.VMEM((count, 2, 2, rows + LAYERS * (LAGS - 2), QUAD * PIECE), BF16),
        ]

    middle_slope = call(
        slope_middle_kernel,
        "slope_middle",
        [VMEM] * 5,
        shaped(len(MIDDLE_SLOPES), SLOPE_ROWS, QUAD * PIECE),
        work(len(MIDDLE_SLOPES), DENSITY_QUADS, SLOPE_ROWS),
        12,
        1e11,
        300,
    )(tiles, *halo_rows, high, low)
    outer_slope = call(
        slope_sides_kernel,
        "slope_sides",
        [VMEM] * 7,
        shaped(2, SLOPE_ROWS, QUAD * PIECE),
        work(2, DENSITY_QUADS, SLOPE_ROWS),
        8,
        2.6e9,
        4,
    )(tiles, *halo_rows, *columns, high, low)

    own_frame = pltpu.VMEM((3, GROUP_ROWS * LAYERS, LANES), F32)
    packed = shaped(side_size(OUTER_SIDE), LANES)
    own_columns = call(columns_kernel, "columns", [VMEM] * 3, [packed, packed], [own_frame], 4, 0, 4)(frame, *own_rows)
    own_columns = exchange_both(own_columns, "gy")

    middle, frame = call(
        gradient_middle_kernel,
        "gradient_middle",
        [VMEM] * 8,
        [shaped(len(MIDDLE) * GRADIENT_ROWS, QUAD * PIECE), shaped(3, GROUP_ROWS * LAYERS, LANES)],
        work(len(MIDDLE), GRADIENT_QUADS, GRADIENT_ROWS),
        8,
        1e9,
        4,
    )(frame, *own_rows, *columns, middle_slope, high, low)
    return call(
        gradient_sides_kernel,
        "gradient_sides",
        [VMEM] * 8,
        shaped(*density.shape),
        [own_frame] + work(4, GRADIENT_QUADS, GRADIENT_ROWS) + [pltpu.VMEM((4 * GRADIENT_ROWS, QUAD * PIECE), F32)],
        12,
        2e9,
        4,
    )(frame, *own_columns, middle_slope, outer_slope, middle, high, low)


def solution(mesh):
    placed = (
        P(None, None, None, None, "gx", "gy"),
        P(None, None, None, None, "gx", "gy"),
        P(),
        P(None, "gx", "gy"),
        P(),
        P(),
    )
    return jax.shard_map(body, mesh=mesh, in_specs=placed, out_specs=P(None, "gx", "gy"), check_vma=False)
```
